256 devices in a mesh: sta: 128 (over y, z, x_lo, core), win: 2 (over x_hi).
Axes of the slice: x: 4 (x_hi: 2, x_lo: 2; x = x_hi * 2 + x_lo), y: 4, z: 8, core: 2. Of those that a mesh axis runs over, the one named last changes fastest.
Arguments:
- traces: float32 [256, 4800], P('sta', 'win'), may hold values from -6 to 6
- response_re: float32 [128, 1024], P('sta'), may hold values from -6 to 6
- response_im: float32 [128, 1024], P('sta'), may hold values from -6 to 6
- station_net: int32 [256], P('sta'), may hold values from 0 to 127
- quality: int32 [256, 4], P('sta', 'win'), may hold values 0 or 1
Outputs:
- correlations: float32 [256, 256, 801], P('sta', 'win')
The draws below stay inside these ranges and needn't reach their ends.
All inputs are finite; a program needn't handle non-finite values. No bound on the sum of `quality` on one device may be relied on, other than what follows from the above.
Results may differ from the reference program's by a relative error of at most 0.0038.
Values may be sent and summed in bfloat16 or wider, within the bound.
A program may use at most 64 MiB of HBM per device.

```python
import math
import jax
import jax.numpy as jnp
import numpy as np
from jax import lax

SEG = 1200
BINS = 1024
MAXLAG = 400
STATIONS = 256
SEGS = 4
NETS = 128


def with_ends(result, rng, smallest, high):
    spot = [jax.random.randint(jax.random.fold_in(rng, axis), (), 0, length) for axis, length in enumerate(result.shape)]
    widest = result.shape.index(max(result.shape))
    next_to = spot[:widest] + [(spot[widest] + 1) % result.shape[widest]] + spot[widest + 1:]
    return result.at[tuple(spot)].set(smallest).at[tuple(next_to)].set(high)


def steps_of(stream_key, dims, pieces, low, top_value):
    factor_of, own = 1.0, jax.random.fold_in(stream_key, 6)
    for position, parts in pieces:
        heights = jnp.exp(jax.random.uniform(jax.random.fold_in(own, position), (parts,), jnp.float32, low / len(pieces), top_value / len(pieces)))
        factor_of = factor_of * jnp.repeat(heights, dims[position] // parts).reshape([-1 if axis == position else 1 for axis in range(len(dims))])
    return factor_of


def rank_bounds(count, lean):
    weights = [(1 << 20) // math.isqrt(standing ** lean) + 1 for standing in range(1, count + 1)]
    spread = 1 + sum(weights) // (1 << 30)
    return np.cumsum(np.array([max(1, weight // spread) for weight in weights]))


def skewed_ids(own_key, extent, number_of, skew):
    grid = rank_bounds(number_of, skew)
    ticket = jax.random.randint(jax.random.fold_in(own_key, 1), extent, 0, int(grid[number_of - 1]))
    standing = jnp.searchsorted(jnp.asarray(grid, jnp.int32), ticket, side="right")
    return jax.random.permutation(jax.random.fold_in(own_key, 2), number_of)[standing].astype(jnp.int32)


def bell_draw(rng, dims, width, most, cuts=(), kind=jnp.bfloat16):
    result = width * jax.random.normal(rng, dims, jnp.float32)
    if cuts:
        result = result * steps_of(rng, dims, cuts, -0.22, 0.18)
    return jnp.clip(result, -most, most).astype(kind)


def setup_inputs(seed: int = 0) -> dict:
    key_list = jax.random.split(jax.random.key(seed), 6)
    return {
        "traces": bell_draw(key_list[0], (STATIONS, SEGS * SEG), 1.0, 6.0, ((0, 128), (1, 2)), jnp.float32),
        "response_re": bell_draw(key_list[1], (NETS, BINS), 1.0, 6.0, ((0, 128),), jnp.float32),
        "response_im": bell_draw(key_list[2], (NETS, BINS), 1.0, 6.0, ((0, 128),), jnp.float32),
        "station_net": with_ends(skewed_ids(key_list[3], (STATIONS,), NETS, 2), jax.random.fold_in(key_list[3], 3), 0, NETS - 1).astype(jnp.int32),
        "quality": with_ends((jax.random.randint(key_list[4], (STATIONS, SEGS), 0, 4) < 3).astype(jnp.int32), jax.random.fold_in(key_list[4], 1), 0, 1),
    }


def forward_table(seg_len, bins):
    times = jnp.arange(seg_len, dtype=jnp.int32)
    freqs = jnp.arange(bins, dtype=jnp.int32)
    phase = times[:, None] * freqs[None, :] % (2 * bins)
    angle = phase.astype(jnp.float32) * (2.0 * math.pi / (2 * bins))
    return jnp.concatenate([jnp.cos(angle), -jnp.sin(angle)], axis=1)

def inverse_table(bins, maxlag):
    freqs = jnp.arange(bins, dtype=jnp.int32)
    shifts = jnp.arange(2 * maxlag + 1, dtype=jnp.int32) - maxlag + 2 * bins
    phase = freqs[:, None] * shifts[None, :] % (2 * bins)
    angle = phase.astype(jnp.float32) * (2.0 * math.pi / (2 * bins))
    weights = jnp.where(freqs == 0, 1.0, 2.0).astype(jnp.float32) / jnp.sqrt(jnp.float32(bins))
    return jnp.concatenate([weights[:, None] * jnp.cos(angle), -weights[:, None] * jnp.sin(angle)], axis=0)

def whiten(rows, resp_re, resp_im, flags, bins):
    spec = jnp.dot(rows, forward_table(rows.shape[1], bins), precision=lax.Precision.HIGHEST, preferred_element_type=jnp.float32)
    spec_re, spec_im = (spec[:, :bins], spec[:, bins:])
    power = resp_re * resp_re + resp_im * resp_im
    level = 0.1 * lax.optimization_barrier(jnp.mean(power, axis=1, keepdims=True)) + 1e-06
    denom = power + level
    dec_re = (spec_re * resp_re + spec_im * resp_im) / denom
    dec_im = (spec_im * resp_re - spec_re * resp_im) / denom
    energy = dec_re * dec_re + dec_im * dec_im
    mean_energy = lax.optimization_barrier(jnp.mean(energy, axis=1, keepdims=True)) + 1e-06
    factor = flags[:, None] / jnp.sqrt(energy + 0.5 * mean_energy)
    return jnp.concatenate([dec_re * factor, dec_im * factor], axis=1).astype(jnp.bfloat16)

def reference(traces, response_re, response_im, station_net, quality):
    stations = traces.shape[0]
    segs = quality.shape[1]
    rows = traces.reshape(stations * segs, SEG)
    resp_re = jnp.repeat(response_re[station_net], segs, axis=0)
    resp_im = jnp.repeat(response_im[station_net], segs, axis=0)
    flags = quality.reshape(-1).astype(jnp.float32)
    white = whiten(rows, resp_re, resp_im, flags, BINS).reshape(stations, segs, 2 * BINS).astype(jnp.float32)
    masks = quality.astype(jnp.float32)
    table = inverse_table(BINS, MAXLAG)
    all_re, all_im = (white[:, :, :BINS], white[:, :, BINS:])

    def one_row(item):
        own, own_mask = item
        own_re, own_im = (own[:, :BINS], own[:, BINS:])
        cross_re = jnp.einsum('sf,jsf->jf', own_re, all_re) + jnp.einsum('sf,jsf->jf', own_im, all_im)
        cross_im = jnp.einsum('sf,jsf->jf', own_im, all_re) - jnp.einsum('sf,jsf->jf', own_re, all_im)
        lags = jnp.dot(jnp.concatenate([cross_re, cross_im], axis=1), table, precision=lax.Precision.HIGHEST, preferred_element_type=jnp.float32)
        count = jnp.dot(masks, own_mask, precision=lax.Precision.HIGHEST, preferred_element_type=jnp.float32)
        return lags / jnp.maximum(count, 1.0)[:, None]
    return lax.map(one_row, (white, masks))
```

```python
import math

import jax
import jax.numpy as jnp
import ml_dtypes
import numpy as np
from jax import lax
from jax.experimental import pallas as pl
from jax.experimental.pallas import tpu as pltpu
from jax.sharding import PartitionSpec as P

MESH = pl.DeviceIdType.MESH
SEG, BINS, MAXLAG = 1200, 1024, 400
FFT = 2 * BINS
LAGS = 2 * MAXLAG + 1
BLOCKS = 7
CHUNKS = ((0, 2), (2, 2), (4, 2), (6, 1))
HIGHEST = lax.Precision.HIGHEST


def tables():
    f1 = np.arange(16)
    lane = np.arange(64)
    f2 = 8 * (lane % 8) + lane // 8
    r = np.arange(128)
    ang = 2 * np.pi * (f1[:, None] * r[None, :] % FFT) / FFT
    twiddle = np.stack([np.cos(ang), -np.sin(ang)]).astype(np.float32)
    ang = 2 * np.pi * (r[:, None] * f2[None, :] % 128) / 128
    c, s = np.cos(ang), np.sin(ang)
    outer = np.concatenate(
        [np.concatenate([c, -s], 1), np.concatenate([s, c], 1)], 0
    ).astype(np.float32)
    f = f1[:, None] + 16 * f2[None, :]
    k = np.arange(LAGS) - MAXLAG
    ang = 2 * np.pi * (f[:, :, None] * k % FFT) / FFT
    w = np.where(f == 0, 1.0, 2.0)[:, :, None] / math.sqrt(BINS)
    inverse = np.zeros((16, 128, BLOCKS * 128), np.float64)
    inverse[:, :64, :LAGS] = w * np.cos(ang)
    inverse[:, 64:, :LAGS] = -w * np.sin(ang)
    return twiddle, outer, inverse.reshape(FFT, BLOCKS * 128).astype(ml_dtypes.bfloat16)


def coords():
    s = lax.axis_index("sta")
    return s // 32, s // 4 % 8, s // 2 % 2, s % 2, lax.axis_index("win")


def device(y, z, xl, c, xh):
    return {"sta": ((y * 8 + z) * 2 + xl) * 2 + c, "win": xh}


def kernel(
    net_ref, qual_ref, tr_ref, re_ref, im_ref, tw_ref, outer_ref, inv_hbm, out_ref,
    inv, xs, lhs, xscr, sq, gbuf, nbuf, csend, crecv, abuf, bbuf, bf, qa, scale, cross, mat, sbuf,
    tsem, s_r1, r_r1, s_n, r_n, s_d, r_d, s_r2, r_r2, s_a, r_a, s_b, r_b, s_o, r_o,
):
    y, z, xl, c, xh = coords()
    me = y * 2 + xl
    lane = lax.broadcasted_iota(jnp.int32, (16, 128), 1)
    low = lane < 64

    def swap(v):
        return pltpu.roll(v, 64, 1)

    def plane(p):
        return device(p // 2, z, p % 2, c, xh)

    def across(p):
        return device(p // 2, z, p % 2, c, 1 - xh)

    half = y // 2
    y_to = y + c * (3 - 2 * y)
    core_to = (1 + xh + half) % 2
    c_from = (y // 2 + xh) % 2
    y_from = y + c_from * (3 - 2 * y)
    xh_from = (1 + c + xh) % 2

    def slot_of(p):
        cb = (p // 4 + xh) % 2
        yb = p // 2 + cb * (3 - 2 * (p // 2))
        return (yb % 2) * 4 + p % 2 * 2 + cb

    barrier = pltpu.get_barrier_semaphore()

    def greet(to):
        pl.semaphore_signal(barrier, inc=1, device_id=to, device_id_type=MESH)

    for d in range(1, 8):
        greet(device(y, (z + d) % 8, xl, c, xh))
        greet(plane((me + d) % 8))
    for d in range(8):
        greet(across((me + d) % 8))
        greet(device(y_from, (z + d) % 8, xl, c_from, xh_from))
    greet(device(y, z, xl, 1 - c, xh))

    table = pltpu.make_async_copy(inv_hbm, inv, tsem)
    table.start()

    sq[...] = jnp.zeros((128, 128), jnp.float32)
    for j in range(8):
        sq[j : j + 1, :] = re_ref[:, 128 * j : 128 * j + 128]
        sq[64 + j : 65 + j, :] = im_ref[:, 128 * j : 128 * j + 128]
    turned = sq[...].T
    resp = turned[0:16, :]
    for m in range(1, 8):
        resp = resp + pltpu.roll(turned[16 * m : 16 * m + 16, :], 8 * m, 1)
    square = resp * resp
    power = square + swap(square)
    level = 0.1 * (jnp.sum(square) / BINS) + 1e-06
    gbuf[c, z] = jnp.where(low, resp, -resp) / (power + level)

    row = lax.broadcasted_iota(jnp.int32, (8, 128), 0)
    nbuf[me] = jnp.where(row < 4, net_ref[0], net_ref[1])

    for q in range(10):
        n = min(128, SEG - 128 * q)
        xs[q] = jnp.zeros((8, 128), jnp.float32)
        xs[q, 0:2, 0:n] = tr_ref[:, 128 * q : 128 * q + n]
        xs[q, 2:4, 0:n] = tr_ref[:, SEG + 128 * q : SEG + 128 * q + n]
    for f in range(9):
        parts = []
        for fn, sign in ((math.cos, 1.0), (math.sin, -1.0)):
            total = jnp.zeros((8, 128), jnp.float32)
            for q in range(10):
                w = sign * fn(2 * math.pi * (f * q % 16) / 16)
                if abs(w) > 1e-9:
                    total = total + (xs[q] if w == 1.0 else xs[q] * w)
            parts.append(total)
        for g in {f, (16 - f) % 16}:
            ar, ai = parts if g == f else (parts[0], -parts[1])
            tr, ti = tw_ref[0, g : g + 1, :], tw_ref[1, g : g + 1, :]
            lhs[8 * g : 8 * g + 8, 0:128] = ar * tr - ai * ti
            lhs[8 * g : 8 * g + 8, 128:256] = ar * ti + ai * tr
    xscr[...] = jnp.dot(
        lhs[...], outer_ref[...], precision=HIGHEST, preferred_element_type=jnp.float32
    )

    pl.semaphore_wait(barrier, 31)

    def remote(src, dst, ssem, rsem, to):
        return pltpu.make_async_remote_copy(
            src_ref=src, dst_ref=dst, send_sem=ssem, recv_sem=rsem, device_id=to,
            device_id_type=MESH,
        )

    sent = []

    def start(copy):
        copy.start()
        sent.append(copy)

    sibling = device(y, z, xl, 1 - c, xh)
    for d in range(1, 8):
        zz = (z + d) % 8
        start(
            remote(gbuf.at[c, z], gbuf.at[c, z], s_r1.at[zz], r_r1.at[z],
                   device(y, zz, xl, c, xh))
        )
    for d in range(1, 8):
        p = (me + d) % 8
        start(remote(nbuf.at[me], nbuf.at[me], s_n.at[p], r_n.at[me], plane(p)))
    for d in range(1, 8):
        zz = (z + d) % 8
        remote(gbuf.at[c, zz], gbuf.at[c, zz], s_r1.at[zz], r_r1.at[zz], sibling).wait_recv()
    start(remote(gbuf.at[c], gbuf.at[c], s_d.at[0], r_d.at[0], sibling))
    for d in range(1, 8):
        p = (me + d) % 8
        remote(nbuf.at[p], nbuf.at[p], s_n.at[p], r_n.at[p], plane(p)).wait_recv()
    remote(gbuf.at[1 - c], gbuf.at[1 - c], s_d.at[0], r_d.at[0], sibling).wait_recv()

    base = y * 32 + xl * 2

    def choose(p):
        want = [nbuf[p, 4 * st : 4 * st + 1, :] for st in range(2)]
        acc = [jnp.zeros((16, 128), jnp.float32) for _ in range(2)]
        for cc in range(2):
            for zz in range(8):
                v = gbuf[cc, zz]
                for st in range(2):
                    acc[st] = jnp.where(want[st] == base + 4 * zz + cc, v, acc[st])
        return acc

    for d in range(1, 8):
        p = (me + d) % 8
        acc = choose(p)
        csend[p, 0], csend[p, 1] = acc[0], acc[1]
        start(remote(csend.at[p], crecv.at[me], s_r2.at[p], r_r2.at[me], plane(p)))
    factors = choose(me)
    for d in range(1, 8):
        p = (me + d) % 8
        remote(csend.at[p], crecv.at[p], s_r2.at[p], r_r2.at[p], plane(p)).wait_recv()
        for st in range(2):
            factors[st] = factors[st] + crecv[p, st]

    own = y * 4 + xh * 2 + xl
    row = lax.broadcasted_iota(jnp.int32, (16, 128), 0)
    marks = jnp.zeros((16, 128), jnp.float32)
    for st in range(2):
        fac = factors[st]
        turn = swap(fac)
        f_re = jnp.where(low, fac, turn)
        f_im = jnp.where(low, -turn, fac)
        for g in range(2):
            spec = xscr[pl.ds(2 * g + st, 16, stride=8), :]
            dec = spec * f_re + swap(spec) * f_im
            square = dec * dec
            energy = square + swap(square)
            mean = jnp.sum(square) / BINS + 1e-06
            flag = qual_ref[st, g].astype(jnp.float32)
            white = dec * (flag / jnp.sqrt(energy + 0.5 * mean))
            abuf[own, 2 * st + g] = white.astype(jnp.bfloat16)
            marks = jnp.where(row // 4 == 2 * st + g, flag, marks)
    abuf[own, 4] = marks.astype(jnp.bfloat16)

    for d in range(8):
        zz = (z + d) % 8
        start(
            remote(abuf.at[own], bbuf.at[xh, z], s_b.at[zz], r_b.at[z],
                   device(y_to, zz, xl, core_to, half))
        )
    for d in range(8):
        p = (me + d) % 8
        if d > 0:
            start(
                remote(abuf.at[own], abuf.at[own], s_a.at[p // 2 * 4 + xh * 2 + p % 2], r_a.at[own],
                       plane(p))
            )
        start(
            remote(abuf.at[own], abuf.at[own], s_a.at[p // 2 * 4 + (1 - xh) * 2 + p % 2],
                   r_a.at[own], across(p))
        )
    for zz in range(8):
        remote(abuf.at[own], bbuf.at[xh_from, zz], s_b.at[zz], r_b.at[zz], sibling).wait_recv()
    start(remote(bbuf.at[xh_from], bbuf.at[xh_from], s_d.at[1], r_d.at[1], sibling))
    for d in range(1, 16):
        s = (own + d) % 16
        remote(abuf.at[own], abuf.at[s], s_a.at[s], r_a.at[s], sibling).wait_recv()
    for p in range(8):
        for x in range(2):
            mark = abuf[p // 2 * 4 + x * 2 + p % 2, 4].astype(jnp.float32)
            for st in range(2):
                for g in range(2):
                    i = 4 * (2 * st + g)
                    qa[2 * x + g, 2 * p + st : 2 * p + st + 1, :] = mark[i : i + 1, :]
    remote(bbuf.at[1 - xh_from], bbuf.at[1 - xh_from], s_d.at[1], r_d.at[1], sibling).wait_recv()

    def second(zz, _):
        marks = [bbuf[x, zz, 4].astype(jnp.float32) for x in range(2)]
        for st in range(2):
            count = jnp.zeros((16, 128), jnp.float32)
            for x in range(2):
                for g in range(2):
                    v = bbuf[x, zz, 2 * st + g].astype(jnp.float32)
                    bf[st * 8 + zz, 2 * x + g, 0] = v
                    bf[st * 8 + zz, 2 * x + g, 1] = swap(v)
                    i = 4 * (2 * st + g)
                    count = count + qa[2 * x + g] * marks[x][i : i + 1, :]
            scale[st * 8 + zz] = 1.0 / jnp.maximum(count, 1.0)
        return 0

    lax.fori_loop(0, 8, second, 0)

    def first(p, _):
        forms = []
        for st in range(2):
            for x in range(2):
                for g in range(2):
                    v = abuf[p // 2 * 4 + x * 2 + p % 2, 2 * st + g].astype(jnp.float32)
                    t = swap(v)
                    forms.append((jnp.where(low, v, -t), jnp.where(low, t, v)))

        def pair(b, _):
            acc = [None, None]
            for s in range(4):
                v, t = bf[b, s, 0], bf[b, s, 1]
                for st in range(2):
                    u, w = forms[4 * st + s]
                    term = u * v + w * t
                    acc[st] = term if acc[st] is None else acc[st] + term
            for st in range(2):
                a = 2 * p + st
                at = pl.multiple_of((a * 16 + b) * 16, 16)
                cross[pl.ds(at, 16), :] = acc[st] * scale[b, pl.ds(a, 1), :]
            return 0

        lax.fori_loop(0, 16, pair, 0, unroll=2)
        return 0

    lax.fori_loop(0, 8, first, 0)
    for f in range(16):
        mat[:, 128 * f : 128 * f + 128] = cross[pl.ds(f, 256, stride=16), :].astype(jnp.bfloat16)

    table.wait()
    mine = slot_of(me)
    for i, (n, count) in enumerate(CHUNKS):
        lags = jnp.dot(
            mat[...], inv[:, 128 * n : 128 * (n + count)], preferred_element_type=jnp.float32
        ).astype(jnp.bfloat16)
        for p in range(8):
            for k in range(count):
                sbuf[p, n + k] = lags[32 * p : 32 * p + 32, 128 * k : 128 * k + 128]
        for d in range(1, 8):
            p = (me + d) % 8
            start(
                remote(sbuf.at[p, pl.ds(n, count)], out_ref.at[mine, pl.ds(n, count)],
                       s_o.at[i, p], r_o.at[i, mine], plane(p))
            )
    keep = pltpu.make_async_copy(sbuf.at[me], out_ref.at[mine], tsem)
    keep.start()
    for i, (n, count) in enumerate(CHUNKS):
        for d in range(1, 8):
            p = (me + d) % 8
            s = slot_of(p)
            remote(sbuf.at[p, pl.ds(n, count)], out_ref.at[s, pl.ds(n, count)],
                   s_o.at[i, p], r_o.at[i, s], plane(p)).wait_recv()
    keep.wait()
    for copy in sent:
        copy.wait_send()


def place(lags_ref, out_ref, rows):
    for n in range(BLOCKS):
        width = min(128, LAGS - 128 * n)
        for a in range(2):
            for s in range(8):
                for st in range(2):
                    at = s // 4 * 64 + s // 2 % 2 * 4 + s % 2 * 2 + st
                    v = lags_ref[s, n, 16 * a + 8 * st : 16 * a + 8 * st + 8, :]
                    rows[pl.ds((2 * n + a) * 128 + at, 8, stride=8), :] = v.astype(jnp.float32)
            v = rows[(2 * n + a) * 128 : (2 * n + a + 1) * 128, :]
            out_ref[a, :, 128 * n : 128 * n + width] = v[:, :width]


def on_device(traces, response_re, response_im, station_net, quality):
    twiddle, outer, inverse = tables()
    f32, bf16 = jnp.float32, jnp.bfloat16
    vmem = pl.BlockSpec(memory_space=pltpu.VMEM)
    smem = pl.BlockSpec(memory_space=pltpu.SMEM)
    dma = pltpu.SemaphoreType.DMA
    lags = pl.pallas_call(
        kernel,
        out_shape=jax.ShapeDtypeStruct((8, BLOCKS, 32, 128), bf16),
        in_specs=[smem, smem, vmem, vmem, vmem, vmem, vmem, pl.BlockSpec(memory_space=pl.ANY)],
        out_specs=pl.BlockSpec(memory_space=pl.ANY),
        scratch_shapes=[
            pltpu.VMEM((FFT, BLOCKS * 128), bf16),
            pltpu.VMEM((10, 8, 128), f32),
            pltpu.VMEM((128, 256), f32),
            pltpu.VMEM((128, 128), f32),
            pltpu.VMEM((128, 128), f32),
            pltpu.VMEM((2, 8, 16, 128), f32),
            pltpu.VMEM((8, 8, 128), jnp.int32),
            pltpu.VMEM((8, 2, 16, 128), f32),
            pltpu.VMEM((8, 2, 16, 128), f32),
            pltpu.VMEM((16, 5, 16, 128), bf16),
            pltpu.VMEM((2, 8, 5, 16, 128), bf16),
            pltpu.VMEM((16, 4, 2, 16, 128), f32),
            pltpu.VMEM((4, 16, 128), f32),
            pltpu.VMEM((16, 16, 128), f32),
            pltpu.VMEM((4096, 128), f32),
            pltpu.VMEM((256, FFT), bf16),
            pltpu.VMEM((8, BLOCKS, 32, 128), bf16),
            dma,
            dma((8,)), dma((8,)), dma((8,)), dma((8,)), dma((2,)), dma((2,)), dma((8,)), dma((8,)),
            dma((16,)), dma((16,)), dma((8,)), dma((8,)), dma((4, 8)), dma((4, 8)),
        ],
        compiler_params=pltpu.CompilerParams(
            collective_id=0, has_side_effects=True, vmem_limit_bytes=40 << 20
        ),
    )(
        station_net, quality, traces, response_re, response_im,
        jnp.asarray(twiddle), jnp.asarray(outer), jnp.asarray(inverse),
    )
    return pl.pallas_call(
        place,
        out_shape=jax.ShapeDtypeStruct((2, 128, LAGS), f32),
        in_specs=[vmem],
        out_specs=vmem,
        scratch_shapes=[pltpu.VMEM((2 * BLOCKS * 128, 128), f32)],
        compiler_params=pltpu.CompilerParams(vmem_limit_bytes=16 << 20),
    )(lags)


def solution(mesh):
    return jax.shard_map(
        on_device,
        mesh=mesh,
        in_specs=(P("sta", "win"), P("sta", None), P("sta", None), P("sta"), P("sta", "win")),
        out_specs=P("sta", "win", None),
        check_vma=False,
    )
```

```python
import math

import jax
import jax.numpy as jnp
import ml_dtypes
import numpy as np
from jax import lax
from jax.experimental import pallas as pl
from jax.experimental.pallas import tpu as pltpu
from jax.sharding import PartitionSpec as P

MESH = pl.DeviceIdType.MESH
SEG, BINS, MAXLAG = 1200, 1024, 400
FFT = 2 * BINS
LAGS = 2 * MAXLAG + 1
BLOCKS = 7
CHUNKS = ((0, 2), (2, 2), (4, 2), (6, 1))
HIGHEST = lax.Precision.HIGHEST


def tables():
    f1 = np.arange(16)
    lane = np.arange(64)
    f2 = 8 * (lane % 8) + lane // 8
    r = np.arange(128)
    ang = 2 * np.pi * (f1[:, None] * r[None, :] % FFT) / FFT
    twiddle = np.stack([np.cos(ang), -np.sin(ang)]).astype(np.float32)
    ang = 2 * np.pi * (r[:, None] * f2[None, :] % 128) / 128
    c, s = np.cos(ang), np.sin(ang)
    outer = np.concatenate(
        [np.concatenate([c, -s], 1), np.concatenate([s, c], 1)], 0
    ).astype(np.float32)
    f = f1[:, None] + 16 * f2[None, :]
    k = np.arange(LAGS) - MAXLAG
    ang = 2 * np.pi * (f[:, :, None] * k % FFT) / FFT
    w = np.where(f == 0, 1.0, 2.0)[:, :, None] / math.sqrt(BINS)
    inverse = np.zeros((16, 128, BLOCKS * 128), np.float64)
    inverse[:, :64, :LAGS] = w * np.cos(ang)
    inverse[:, 64:, :LAGS] = -w * np.sin(ang)
    return twiddle, outer, inverse.reshape(FFT, BLOCKS * 128).astype(ml_dtypes.bfloat16)


def coords():
    s = lax.axis_index("sta")
    return s // 32, s // 4 % 8, s // 2 % 2, s % 2, lax.axis_index("win")


def device(y, z, xl, c, xh):
    return {"sta": ((y * 8 + z) * 2 + xl) * 2 + c, "win": xh}


def kernel(
    net_hbm, qual_hbm, tr_hbm, re_hbm, im_hbm, tw_hbm, outer_hbm, inv_hbm, out_ref,
    net_ref, qual_ref, tr_ref, re_ref, im_ref, tw_ref, outer_ref, inv, xs, lhs, xscr, sq, gbuf, nbuf, csend, crecv, abuf, bbuf, bf, qa, scale, cross, mat, sbuf,
    isem, tsem, s_r1, r_r1, s_n, r_n, s_d, r_d, s_r2, r_r2, s_a, r_a, s_b, r_b, s_o, r_o,
):
    y, z, xl, c, xh = coords()
    me = y * 2 + xl
    lane = lax.broadcasted_iota(jnp.int32, (16, 128), 1)
    low = lane < 64

    def swap(v):
        return pltpu.roll(v, 64, 1)

    def plane(p):
        return device(p // 2, z, p % 2, c, xh)

    def across(p):
        return device(p // 2, z, p % 2, c, 1 - xh)

    half = y // 2
    y_to = y + c * (3 - 2 * y)
    core_to = (1 + xh + half) % 2
    c_from = (y // 2 + xh) % 2
    y_from = y + c_from * (3 - 2 * y)
    xh_from = (1 + c + xh) % 2

    def slot_of(p):
        cb = (p // 4 + xh) % 2
        yb = p // 2 + cb * (3 - 2 * (p // 2))
        return (yb % 2) * 4 + p % 2 * 2 + cb

    loads = [
        pltpu.make_async_copy(src, dst, isem.at[i])
        for i, (src, dst) in enumerate(
            (
                (re_hbm, re_ref), (im_hbm, im_ref), (tr_hbm, tr_ref), (net_hbm, net_ref),
                (qual_hbm, qual_ref), (tw_hbm, tw_ref), (outer_hbm, outer_ref),
            )
        )
    ]
    for load in loads:
        load.start()

    barrier = pltpu.get_barrier_semaphore()

    def greet(to):
        pl.semaphore_signal(barrier, inc=1, device_id=to, device_id_type=MESH)

    for d in range(1, 8):
        greet(device(y, (z + d) % 8, xl, c, xh))
        greet(plane((me + d) % 8))
    greet(device(y, z, xl, 1 - c, xh))
    greet(across(me))

    table = pltpu.make_async_copy(inv_hbm, inv, tsem)
    table.start()

    for load in loads:
        load.wait()
    sq[...] = jnp.zeros((128, 128), jnp.float32)
    for j in range(8):
        sq[j : j + 1, :] = re_ref[:, 128 * j : 128 * j + 128]
        sq[64 + j : 65 + j, :] = im_ref[:, 128 * j : 128 * j + 128]
    turned = sq[...].T
    resp = turned[0:16, :]
    for m in range(1, 8):
        resp = resp + pltpu.roll(turned[16 * m : 16 * m + 16, :], 8 * m, 1)
    square = resp * resp
    power = square + swap(square)
    level = 0.1 * (jnp.sum(square) / BINS) + 1e-06
    gbuf[c, z] = jnp.where(low, resp, -resp) / (power + level)

    row = lax.broadcasted_iota(jnp.int32, (8, 128), 0)
    nbuf[me] = jnp.where(row < 4, net_ref[0], net_ref[1])

    for q in range(10):
        n = min(128, SEG - 128 * q)
        xs[q] = jnp.zeros((8, 128), jnp.float32)
        xs[q, 0:2, 0:n] = tr_ref[:, 128 * q : 128 * q + n]
        xs[q, 2:4, 0:n] = tr_ref[:, SEG + 128 * q : SEG + 128 * q + n]
    for f in range(9):
        parts = []
        for fn, sign in ((math.cos, 1.0), (math.sin, -1.0)):
            total = jnp.zeros((8, 128), jnp.float32)
            for q in range(10):
                w = sign * fn(2 * math.pi * (f * q % 16) / 16)
                if abs(w) > 1e-9:
                    total = total + (xs[q] if w == 1.0 else xs[q] * w)
            parts.append(total)
        for g in {f, (16 - f) % 16}:
            ar, ai = parts if g == f else (parts[0], -parts[1])
            tr, ti = tw_ref[0, g : g + 1, :], tw_ref[1, g : g + 1, :]
            lhs[8 * g : 8 * g + 8, 0:128] = ar * tr - ai * ti
            lhs[8 * g : 8 * g + 8, 128:256] = ar * ti + ai * tr
    xscr[...] = jnp.dot(
        lhs[...], outer_ref[...], precision=HIGHEST, preferred_element_type=jnp.float32
    )

    pl.semaphore_wait(barrier, 16)

    def remote(src, dst, ssem, rsem, to):
        return pltpu.make_async_remote_copy(
            src_ref=src, dst_ref=dst, send_sem=ssem, recv_sem=rsem, device_id=to,
            device_id_type=MESH,
        )

    sent = []

    def start(copy):
        copy.start()
        sent.append(copy)

    sibling = device(y, z, xl, 1 - c, xh)
    for d in range(1, 8):
        zz = (z + d) % 8
        start(
            remote(gbuf.at[c, z], gbuf.at[c, z], s_r1.at[zz], r_r1.at[z],
                   device(y, zz, xl, c, xh))
        )
    for d in range(1, 8):
        p = (me + d) % 8
        start(remote(nbuf.at[me], nbuf.at[me], s_n.at[p], r_n.at[me], plane(p)))
    for d in range(1, 8):
        zz = (z + d) % 8
        remote(gbuf.at[c, zz], gbuf.at[c, zz], s_r1.at[zz], r_r1.at[zz], sibling).wait_recv()
    start(remote(gbuf.at[c], gbuf.at[c], s_d.at[0], r_d.at[0], sibling))
    for d in range(1, 8):
        p = (me + d) % 8
        remote(nbuf.at[p], nbuf.at[p], s_n.at[p], r_n.at[p], plane(p)).wait_recv()
    remote(gbuf.at[1 - c], gbuf.at[1 - c], s_d.at[0], r_d.at[0], sibling).wait_recv()

    base = y * 32 + xl * 2

    def choose(p):
        want = [nbuf[p, 4 * st : 4 * st + 1, :] for st in range(2)]
        acc = [jnp.zeros((16, 128), jnp.float32) for _ in range(2)]
        for cc in range(2):
            for zz in range(8):
                v = gbuf[cc, zz]
                for st in range(2):
                    acc[st] = jnp.where(want[st] == base + 4 * zz + cc, v, acc[st])
        return acc

    for d in range(1, 8):
        p = (me + d) % 8
        acc = choose(p)
        csend[p, 0], csend[p, 1] = acc[0], acc[1]
        start(remote(csend.at[p], crecv.at[me], s_r2.at[p], r_r2.at[me], plane(p)))
    factors = choose(me)
    for d in range(1, 8):
        p = (me + d) % 8
        remote(csend.at[p], crecv.at[p], s_r2.at[p], r_r2.at[p], plane(p)).wait_recv()
        for st in range(2):
            factors[st] = factors[st] + crecv[p, st]

    own = y * 4 + xh * 2 + xl
    row = lax.broadcasted_iota(jnp.int32, (16, 128), 0)
    marks = jnp.zeros((16, 128), jnp.float32)
    for st in range(2):
        fac = factors[st]
        turn = swap(fac)
        f_re = jnp.where(low, fac, turn)
        f_im = jnp.where(low, -turn, fac)
        for g in range(2):
            spec = xscr[pl.ds(2 * g + st, 16, stride=8), :]
            dec = spec * f_re + swap(spec) * f_im
            square = dec * dec
            energy = square + swap(square)
            mean = jnp.sum(square) / BINS + 1e-06
            flag = qual_ref[st, g].astype(jnp.float32)
            white = dec * (flag / jnp.sqrt(energy + 0.5 * mean))
            abuf[own, 2 * st + g] = white.astype(jnp.bfloat16)
            marks = jnp.where(row // 4 == 2 * st + g, flag, marks)
    abuf[own, 4] = marks.astype(jnp.bfloat16)

    for d in range(8):
        zz = (z + d) % 8
        start(
            remote(abuf.at[own], bbuf.at[xh, z], s_b.at[zz], r_b.at[z],
                   device(y_to, zz, xl, core_to, half))
        )
    for d in range(8):
        p = (me + d) % 8
        if d > 0:
            start(
                remote(abuf.at[own], abuf.at[own], s_a.at[p // 2 * 4 + xh * 2 + p % 2], r_a.at[own],
                       plane(p))
            )
        start(
            remote(abuf.at[own], abuf.at[own], s_a.at[p // 2 * 4 + (1 - xh) * 2 + p % 2],
                   r_a.at[own], across(p))
        )
    for zz in range(8):
        remote(abuf.at[own], bbuf.at[xh_from, zz], s_b.at[zz], r_b.at[zz], sibling).wait_recv()
    start(remote(bbuf.at[xh_from], bbuf.at[xh_from], s_d.at[1], r_d.at[1], sibling))
    for d in range(1, 16):
        s = (own + d) % 16
        remote(abuf.at[own], abuf.at[s], s_a.at[s], r_a.at[s], sibling).wait_recv()
    for p in range(8):
        for x in range(2):
            mark = abuf[p // 2 * 4 + x * 2 + p % 2, 4].astype(jnp.float32)
            for st in range(2):
                for g in range(2):
                    i = 4 * (2 * st + g)
                    qa[2 * x + g, 2 * p + st : 2 * p + st + 1, :] = mark[i : i + 1, :]
    remote(bbuf.at[1 - xh_from], bbuf.at[1 - xh_from], s_d.at[1], r_d.at[1], sibling).wait_recv()

    def second(zz, _):
        marks = [bbuf[x, zz, 4].astype(jnp.float32) for x in range(2)]
        for st in range(2):
            count = jnp.zeros((16, 128), jnp.float32)
            for x in range(2):
                for g in range(2):
                    v = bbuf[x, zz, 2 * st + g].astype(jnp.float32)
                    bf[st * 8 + zz, 2 * x + g, 0] = v
                    bf[st * 8 + zz, 2 * x + g, 1] = swap(v)
                    i = 4 * (2 * st + g)
                    count = count + qa[2 * x + g] * marks[x][i : i + 1, :]
            scale[st * 8 + zz] = 1.0 / jnp.maximum(count, 1.0)
        return 0

    lax.fori_loop(0, 8, second, 0)

    def first(p, _):
        forms = []
        for st in range(2):
            for x in range(2):
                for g in range(2):
                    v = abuf[p // 2 * 4 + x * 2 + p % 2, 2 * st + g].astype(jnp.float32)
                    t = swap(v)
                    forms.append((jnp.where(low, v, -t), jnp.where(low, t, v)))

        def pair(b, _):
            acc = [None, None]
            for s in range(4):
                v, t = bf[b, s, 0], bf[b, s, 1]
                for st in range(2):
                    u, w = forms[4 * st + s]
                    term = u * v + w * t
                    acc[st] = term if acc[st] is None else acc[st] + term
            for st in range(2):
                a = 2 * p + st
                at = pl.multiple_of((a * 16 + b) * 16, 16)
                cross[pl.ds(at, 16), :] = acc[st] * scale[b, pl.ds(a, 1), :]
            return 0

        lax.fori_loop(0, 16, pair, 0, unroll=2)
        return 0

    lax.fori_loop(0, 8, first, 0)
    for f in range(16):
        mat[:, 128 * f : 128 * f + 128] = cross[pl.ds(f, 256, stride=16), :].astype(jnp.bfloat16)

    table.wait()
    mine = slot_of(me)
    for i, (n, count) in enumerate(CHUNKS):
        lags = jnp.dot(
            mat[...], inv[:, 128 * n : 128 * (n + count)], preferred_element_type=jnp.float32
        ).astype(jnp.bfloat16)
        for p in range(8):
            for k in range(count):
                sbuf[p, n + k] = lags[32 * p : 32 * p + 32, 128 * k : 128 * k + 128]
        for d in range(1, 8):
            p = (me + d) % 8
            start(
                remote(sbuf.at[p, pl.ds(n, count)], out_ref.at[mine, pl.ds(n, count)],
                       s_o.at[i, p], r_o.at[i, mine], plane(p))
            )
    keep = pltpu.make_async_copy(sbuf.at[me], out_ref.at[mine], tsem)
    keep.start()
    for i, (n, count) in enumerate(CHUNKS):
        for d in range(1, 8):
            p = (me + d) % 8
            s = slot_of(p)
            remote(sbuf.at[p, pl.ds(n, count)], out_ref.at[s, pl.ds(n, count)],
                   s_o.at[i, p], r_o.at[i, s], plane(p)).wait_recv()
    keep.wait()
    for copy in sent:
        copy.wait_send()


def place(lags_ref, out_ref, rows):
    for n in range(BLOCKS):
        width = min(128, LAGS - 128 * n)
        for a in range(2):
            for s in range(8):
                for st in range(2):
                    at = s // 4 * 64 + s // 2 % 2 * 4 + s % 2 * 2 + st
                    v = lags_ref[s, n, 16 * a + 8 * st : 16 * a + 8 * st + 8, :]
                    rows[pl.ds((2 * n + a) * 128 + at, 8, stride=8), :] = v.astype(jnp.float32)
            v = rows[(2 * n + a) * 128 : (2 * n + a + 1) * 128, :]
            out_ref[a, :, 128 * n : 128 * n + width] = v[:, :width]


def on_device(traces, response_re, response_im, station_net, quality):
    twiddle, outer, inverse = tables()
    f32, bf16 = jnp.float32, jnp.bfloat16
    vmem = pl.BlockSpec(memory_space=pltpu.VMEM)
    dma = pltpu.SemaphoreType.DMA
    lags = pl.pallas_call(
        kernel,
        out_shape=jax.ShapeDtypeStruct((8, BLOCKS, 32, 128), bf16),
        in_specs=[pl.BlockSpec(memory_space=pltpu.HBM)] * 8,
        out_specs=pl.BlockSpec(memory_space=pl.ANY),
        scratch_shapes=[
            pltpu.SMEM(station_net.shape, jnp.int32),
            pltpu.SMEM(quality.shape, jnp.int32),
            pltpu.VMEM(traces.shape, f32),
            pltpu.VMEM(response_re.shape, f32),
            pltpu.VMEM(response_im.shape, f32),
            pltpu.VMEM(twiddle.shape, f32),
            pltpu.VMEM(outer.shape, f32),
            pltpu.VMEM((FFT, BLOCKS * 128), bf16),
            pltpu.VMEM((10, 8, 128), f32),
            pltpu.VMEM((128, 256), f32),
            pltpu.VMEM((128, 128), f32),
            pltpu.VMEM((128, 128), f32),
            pltpu.VMEM((2, 8, 16, 128), f32),
            pltpu.VMEM((8, 8, 128), jnp.int32),
            pltpu.VMEM((8, 2, 16, 128), f32),
            pltpu.VMEM((8, 2, 16, 128), f32),
            pltpu.VMEM((16, 5, 16, 128), bf16),
            pltpu.VMEM((2, 8, 5, 16, 128), bf16),
            pltpu.VMEM((16, 4, 2, 16, 128), f32),
            pltpu.VMEM((4, 16, 128), f32),
            pltpu.VMEM((16, 16, 128), f32),
            pltpu.VMEM((4096, 128), f32),
            pltpu.VMEM((256, FFT), bf16),
            pltpu.VMEM((8, BLOCKS, 32, 128), bf16),
            dma((7,)), dma,
            dma((8,)), dma((8,)), dma((8,)), dma((8,)), dma((2,)), dma((2,)), dma((8,)), dma((8,)),
            dma((16,)), dma((16,)), dma((8,)), dma((8,)), dma((4, 8)), dma((4, 8)),
        ],
        compiler_params=pltpu.CompilerParams(
            collective_id=0, has_side_effects=True, vmem_limit_bytes=64 << 20
        ),
    )(
        station_net, quality, traces, response_re, response_im,
        jnp.asarray(twiddle), jnp.asarray(outer), jnp.asarray(inverse),
    )
    return pl.pallas_call(
        place,
        out_shape=jax.ShapeDtypeStruct((2, 128, LAGS), f32),
        in_specs=[vmem],
        out_specs=vmem,
        scratch_shapes=[pltpu.VMEM((2 * BLOCKS * 128, 128), f32)],
        compiler_params=pltpu.CompilerParams(vmem_limit_bytes=16 << 20),
    )(lags)


def solution(mesh):
    return jax.shard_map(
        on_device,
        mesh=mesh,
        in_specs=(P("sta", "win"), P("sta", None), P("sta", None), P("sta"), P("sta", "win")),
        out_specs=P("sta", "win", None),
        check_vma=False,
    )
```

```python
import math

import jax
import jax.numpy as jnp
import ml_dtypes
import numpy as np
from jax import lax
from jax.experimental import pallas as pl
from jax.experimental.pallas import tpu as pltpu
from jax.sharding import PartitionSpec as P

MESH = pl.DeviceIdType.MESH
SEG, BINS, MAXLAG = 1200, 1024, 400
FFT = 2 * BINS
LAGS = 2 * MAXLAG + 1
BLOCKS = 7
CHUNKS = ((0, 2), (2, 2), (4, 2), (6, 1))
GROUPS = ((0, 4), (4, 3))
HIGHEST = lax.Precision.HIGHEST


def tables():
    f1 = np.arange(16)
    lane = np.arange(64)
    f2 = 8 * (lane % 8) + lane // 8
    r = np.arange(128)
    ang = 2 * np.pi * (f1[:, None] * r[None, :] % FFT) / FFT
    twiddle = np.stack([np.cos(ang), -np.sin(ang)]).astype(np.float32)
    ang = 2 * np.pi * (r[:, None] * f2[None, :] % 128) / 128
    c, s = np.cos(ang), np.sin(ang)
    outer = np.concatenate(
        [np.concatenate([c, -s], 1), np.concatenate([s, c], 1)], 0
    ).astype(np.float32)
    f = f1[:, None] + 16 * f2[None, :]
    k = np.arange(LAGS) - MAXLAG
    ang = 2 * np.pi * (f[:, :, None] * k % FFT) / FFT
    w = np.where(f == 0, 1.0, 2.0)[:, :, None] / math.sqrt(BINS)
    inverse = np.zeros((16, 128, BLOCKS * 128), np.float64)
    inverse[:, :64, :LAGS] = w * np.cos(ang)
    inverse[:, 64:, :LAGS] = -w * np.sin(ang)
    return twiddle, outer, inverse.reshape(FFT, BLOCKS * 128).astype(ml_dtypes.bfloat16)


def coords():
    s = lax.axis_index("sta")
    return s // 32, s // 4 % 8, s // 2 % 2, s % 2, lax.axis_index("win")


def device(y, z, xl, c, xh):
    return {"sta": ((y * 8 + z) * 2 + xl) * 2 + c, "win": xh}


def kernel(
    net_hbm, qual_hbm, tr_hbm, re_hbm, im_hbm, tw_hbm, outer_hbm, inv_hbm, out_ref,
    net_ref, qual_ref, tr_ref, re_ref, im_ref, tw_ref, outer_ref, inv,
    xs, lhs, xscr, sq, xsend, xrecv, gbuf, nbuf, csend, crecv, fa, fb, abuf, bbuf, bf, qa, scale, cross, mat, sbuf,
    isem, tsem, s_x, r_x, s_r1, r_r1, s_n, r_n, s_d, r_d, s_r2, r_r2, s_fa, r_fa, s_fb, r_fb, s_a, r_a, s_b, r_b,
    s_o, r_o,
):
    y, z, xl, c, xh = coords()
    me = y * 2 + xl
    own = y * 4 + xh * 2 + xl
    lane = lax.broadcasted_iota(jnp.int32, (16, 128), 1)
    low = lane < 64

    def swap(v):
        return pltpu.roll(v, 64, 1)

    def plane(p):
        return device(p // 2, z, p % 2, c, xh)

    def across(p):
        return device(p // 2, z, p % 2, c, 1 - xh)

    def moved(yy, st):
        return yy + (1 - 2 * (yy % 2)) * (1 - st) + (3 - 2 * yy) * st

    def which(yy, hh):
        return (yy // 2 + hh) % 2

    st_own = which(y, xh)
    home = moved(y, st_own)

    def slot_of(p):
        st = which(p // 2, xh)
        return (moved(p // 2, st) % 2) * 4 + p % 2 * 2 + st

    loads = [
        pltpu.make_async_copy(src, dst, isem.at[i])
        for i, (src, dst) in enumerate(
            (
                (re_hbm, re_ref), (im_hbm, im_ref), (tr_hbm, tr_ref), (net_hbm, net_ref),
                (qual_hbm, qual_ref), (tw_hbm, tw_ref), (outer_hbm, outer_ref),
            )
        )
    ]
    for load in loads:
        load.start()

    barrier = pltpu.get_barrier_semaphore()

    def greet(to):
        pl.semaphore_signal(barrier, inc=1, device_id=to, device_id_type=MESH)

    for d in range(1, 8):
        greet(device(y, (z + d) % 8, xl, c, xh))
        greet(plane((me + d) % 8))
    greet(device(y, z, xl, 1 - c, xh))
    greet(device(home, z, xl, c, 0))
    greet(device(home, z, xl, c, 1))

    table = pltpu.make_async_copy(inv_hbm, inv, tsem)
    table.start()

    for load in loads:
        load.wait()
    sq[...] = jnp.zeros((128, 128), jnp.float32)
    for j in range(8):
        sq[j : j + 1, :] = re_ref[:, 128 * j : 128 * j + 128]
        sq[64 + j : 65 + j, :] = im_ref[:, 128 * j : 128 * j + 128]
    turned = sq[...].T
    resp = turned[0:16, :]
    for m in range(1, 8):
        resp = resp + pltpu.roll(turned[16 * m : 16 * m + 16, :], 8 * m, 1)
    square = resp * resp
    power = square + swap(square)
    level = 0.1 * (jnp.sum(square) / BINS) + 1e-06
    gbuf[c, z] = jnp.where(low, resp, -resp) / (power + level)

    row = lax.broadcasted_iota(jnp.int32, (8, 128), 0)
    nbuf[me] = jnp.where(row < 4, net_ref[0], net_ref[1])

    for q in range(10):
        n = min(128, SEG - 128 * q)
        xs[q] = jnp.zeros((8, 128), jnp.float32)
        xs[q, 0:2, 0:n] = tr_ref[:, 128 * q : 128 * q + n]
        xs[q, 2:4, 0:n] = tr_ref[:, SEG + 128 * q : SEG + 128 * q + n]
    for f in range(9):
        parts = []
        for fn, sign in ((math.cos, 1.0), (math.sin, -1.0)):
            total = jnp.zeros((8, 128), jnp.float32)
            for q in range(10):
                w = sign * fn(2 * math.pi * (f * q % 16) / 16)
                if abs(w) > 1e-9:
                    total = total + (xs[q] if w == 1.0 else xs[q] * w)
            parts.append(total)
        for g in {f, (16 - f) % 16}:
            ar, ai = parts if g == f else (parts[0], -parts[1])
            tr, ti = tw_ref[0, g : g + 1, :], tw_ref[1, g : g + 1, :]
            lhs[8 * g : 8 * g + 8, 0:128] = ar * tr - ai * ti
            lhs[8 * g : 8 * g + 8, 128:256] = ar * ti + ai * tr
    xscr[...] = jnp.dot(
        lhs[...], outer_ref[...], precision=HIGHEST, preferred_element_type=jnp.float32
    )
    group = lax.broadcasted_iota(jnp.int32, (8, 128), 1) // 32
    for st in range(2):
        flags = jnp.zeros((8, 128), jnp.float32)
        for g in range(2):
            flag = qual_ref[st, g].astype(jnp.float32)
            xsend[st, 16 * g : 16 * g + 16] = xscr[pl.ds(2 * g + st, 16, stride=8), :] * flag
            flags = jnp.where(group == 2 * xh + g, flag, flags)
        xsend[st, 32:40] = flags

    pl.semaphore_wait(barrier, 17)

    def remote(src, dst, ssem, rsem, to):
        return pltpu.make_async_remote_copy(
            src_ref=src, dst_ref=dst, send_sem=ssem, recv_sem=rsem, device_id=to,
            device_id_type=MESH,
        )

    sent = []

    def start(copy):
        copy.start()
        sent.append(copy)

    sibling = device(y, z, xl, 1 - c, xh)
    for d in (4, 3, 5, 2, 6, 1, 7):
        zz = (z + d) % 8
        start(
            remote(gbuf.at[c, z], gbuf.at[c, z], s_r1.at[zz], r_r1.at[z],
                   device(y, zz, xl, c, xh))
        )
    for st in range(2):
        start(
            remote(xsend.at[st], xrecv.at[xh], s_x.at[st], r_x.at[xh],
                   device(moved(y, st), z, xl, c, y // 2))
        )
    for d in range(1, 8):
        p = (me + d) % 8
        start(remote(nbuf.at[me], nbuf.at[me], s_n.at[p], r_n.at[me], plane(p)))
    for x in range(2):
        remote(xsend.at[0], xrecv.at[x], s_x.at[0], r_x.at[x], sibling).wait_recv()
    mark = xrecv[0, 32:33, :] + xrecv[1, 32:33, :]
    fa[own] = mark
    fb[c, z] = mark
    for d in range(1, 8):
        zz = (z + d) % 8
        remote(gbuf.at[c, zz], gbuf.at[c, zz], s_r1.at[zz], r_r1.at[zz], sibling).wait_recv()
    start(remote(gbuf.at[c], gbuf.at[c], s_d.at[0], r_d.at[0], sibling))
    for d in range(1, 8):
        zz = (z + d) % 8
        start(remote(fb.at[c, z], fb.at[c, z], s_fb.at[zz], r_fb.at[z], device(y, zz, xl, c, xh)))
    for d in range(1, 8):
        p = (me + d) % 8
        remote(nbuf.at[p], nbuf.at[p], s_n.at[p], r_n.at[p], plane(p)).wait_recv()
    remote(gbuf.at[1 - c], gbuf.at[1 - c], s_d.at[0], r_d.at[0], sibling).wait_recv()

    base = y * 32 + xl * 2

    def choose(p):
        st = which(p // 2, xh)
        want = nbuf[moved(p // 2, st) * 2 + p % 2, pl.ds(4 * st, 1), :]
        acc = jnp.zeros((16, 128), jnp.float32)
        for cc in range(2):
            for zz in range(8):
                acc = jnp.where(want == base + 4 * zz + cc, gbuf[cc, zz], acc)
        return acc

    for d in (4, 5, 3, 2, 6, 1, 7):
        p = (me + d) % 8
        csend[p] = choose(p)
        start(remote(csend.at[p], crecv.at[me], s_r2.at[p], r_r2.at[me], plane(p)))
    factor = choose(me)
    specs = [xrecv[x, 16 * g : 16 * g + 16, :] for x in range(2) for g in range(2)]
    turned = [swap(spec) for spec in specs]
    for d in range(1, 8):
        p = (me + d) % 8
        remote(csend.at[p], crecv.at[p], s_r2.at[p], r_r2.at[p], plane(p)).wait_recv()
        factor = factor + crecv[p]

    turn = swap(factor)
    f_re = jnp.where(low, factor, turn)
    f_im = jnp.where(low, -turn, factor)
    for s in range(4):
        dec = specs[s] * f_re + turned[s] * f_im
        square = dec * dec
        energy = square + swap(square)
        mean = jnp.sum(square) / BINS + 1e-06
        abuf[own, s] = (dec / jnp.sqrt(energy + 0.5 * mean)).astype(jnp.bfloat16)

    for d in (4, 3, 5, 2, 6, 1, 7):
        zz = (z + d) % 8
        start(
            remote(abuf.at[own], bbuf.at[c, z], s_b.at[zz], r_b.at[z], device(y, zz, xl, c, xh))
        )
    for d in (4, 5, 3, 2, 6, 1, 7, 0):
        p = (me + d) % 8
        if d > 0:
            start(
                remote(abuf.at[own], abuf.at[own], s_a.at[p // 2 * 4 + xh * 2 + p % 2], r_a.at[own],
                       plane(p))
            )
        start(
            remote(abuf.at[own], abuf.at[own], s_a.at[p // 2 * 4 + (1 - xh) * 2 + p % 2],
                   r_a.at[own], across(p))
        )
    bbuf[c, z] = abuf[own]

    for d in range(8):
        p = (me + d) % 8
        if d > 0:
            start(
                remote(fa.at[own], fa.at[own], s_fa.at[p // 2 * 4 + xh * 2 + p % 2], r_fa.at[own],
                       plane(p))
            )
        start(
            remote(fa.at[own], fa.at[own], s_fa.at[p // 2 * 4 + (1 - xh) * 2 + p % 2], r_fa.at[own],
                   across(p))
        )
    for d in range(1, 8):
        zz = (z + d) % 8
        remote(fb.at[c, z], fb.at[c, zz], s_fb.at[zz], r_fb.at[zz], sibling).wait_recv()
    start(remote(fb.at[c], fb.at[c], s_d.at[1], r_d.at[1], sibling))

    for d in range(1, 8):
        zz = (z + d) % 8
        remote(abuf.at[own], bbuf.at[c, zz], s_b.at[zz], r_b.at[zz], sibling).wait_recv()
    start(remote(bbuf.at[c], bbuf.at[c], s_d.at[2], r_d.at[2], sibling))
    for d in range(1, 16):
        s = (own + d) % 16
        remote(fa.at[own], fa.at[s], s_fa.at[s], r_fa.at[s], sibling).wait_recv()
    remote(fb.at[1 - c], fb.at[1 - c], s_d.at[1], r_d.at[1], sibling).wait_recv()

    def first_slot(i, st):
        p = (me + i + 3) % 8
        return moved(p // 2, st) * 4 + p // 4 * 2 + p % 2

    for i in range(8):
        for st in range(2):
            qa[2 * i + st : 2 * i + st + 1, :] = fa[first_slot(i, st)]
    for cc in range(2):
        for zz in range(8):
            count = qa[...] * fb[cc, zz]
            count = count + swap(count)
            count = count + pltpu.roll(count, 32, 1)
            scale[8 * cc + zz] = 1.0 / jnp.maximum(count, 1.0)

    for d in range(1, 16):
        s = (own + d) % 16
        remote(abuf.at[own], abuf.at[s], s_a.at[s], r_a.at[s], sibling).wait_recv()
    remote(bbuf.at[1 - c], bbuf.at[1 - c], s_d.at[2], r_d.at[2], sibling).wait_recv()

    def second(b, _):
        for s in range(4):
            v = bbuf[b // 8, b % 8, s].astype(jnp.float32)
            bf[b, s, 0] = v
            bf[b, s, 1] = swap(v)
        return 0

    lax.fori_loop(0, 16, second, 0, unroll=2)

    def first(i, _):
        forms = []
        for st in range(2):
            slot = first_slot(i, st)
            for s in range(4):
                v = abuf[slot, s].astype(jnp.float32)
                t = swap(v)
                forms.append((jnp.where(low, v, -t), jnp.where(low, t, v)))

        def pair(b, _):
            acc = [None, None]
            for s in range(4):
                v, t = bf[b, s, 0], bf[b, s, 1]
                for st in range(2):
                    u, w = forms[4 * st + s]
                    term = u * v + w * t
                    acc[st] = term if acc[st] is None else acc[st] + term
            for st in range(2):
                a = 2 * i + st
                at = pl.multiple_of((a * 16 + b) * 16, 16)
                cross[pl.ds(at, 16), :] = acc[st] * scale[b, pl.ds(a, 1), :]
            return 0

        lax.fori_loop(0, 16, pair, 0, unroll=2)
        return 0

    mine = slot_of(me)
    for part in range(2):
        lax.fori_loop(4 * part, 4 * part + 4, first, 0)
        for f in range(16):
            v = cross[pl.ds(2048 * part + f, 128, stride=16), :]
            mat[128 * part : 128 * part + 128, 128 * f : 128 * f + 128] = v.astype(jnp.bfloat16)
        if part == 0:
            table.wait()
        for n, count in CHUNKS:
            lags = jnp.dot(
                mat[128 * part : 128 * part + 128, :],
                inv[:, 128 * n : 128 * (n + count)],
                preferred_element_type=jnp.float32,
            ).astype(jnp.bfloat16)
            for i in range(4):
                for j in range(count):
                    sbuf[4 * part + i, n + j] = lags[
                        32 * i : 32 * i + 32, 128 * j : 128 * j + 128
                    ]
            for k, (at, many) in enumerate(GROUPS):
                if n + count == at + many:
                    for i in range(4 * part, 4 * part + 4):
                        if i != 5:
                            start(
                                remote(sbuf.at[i, pl.ds(at, many)], out_ref.at[mine, pl.ds(at, many)],
                                       s_o.at[k, i], r_o.at[k, mine], plane((me + i + 3) % 8))
                            )
    keep = pltpu.make_async_copy(sbuf.at[5], out_ref.at[mine], tsem)
    keep.start()
    for k, (at, many) in enumerate(GROUPS):
        for d in range(1, 8):
            s = slot_of((me + d) % 8)
            remote(sbuf.at[0, pl.ds(at, many)], out_ref.at[s, pl.ds(at, many)],
                   s_o.at[k, 0], r_o.at[k, s], sibling).wait_recv()
    keep.wait()
    for copy in sent:
        copy.wait_send()


def place(lags_ref, out_ref, rows):
    for n in range(BLOCKS):
        width = min(128, LAGS - 128 * n)
        for a in range(2):
            for s in range(8):
                for st in range(2):
                    at = s // 4 * 64 + s // 2 % 2 * 4 + s % 2 + st * 2
                    v = lags_ref[s, n, 16 * a + 8 * st : 16 * a + 8 * st + 8, :]
                    rows[pl.ds((2 * n + a) * 128 + at, 8, stride=8), :] = v.astype(jnp.float32)
            v = rows[(2 * n + a) * 128 : (2 * n + a + 1) * 128, :]
            out_ref[a, :, 128 * n : 128 * n + width] = v[:, :width]


def on_device(traces, response_re, response_im, station_net, quality):
    twiddle, outer, inverse = tables()
    f32, bf16 = jnp.float32, jnp.bfloat16
    vmem = pl.BlockSpec(memory_space=pltpu.VMEM)
    dma = pltpu.SemaphoreType.DMA
    lags = pl.pallas_call(
        kernel,
        out_shape=jax.ShapeDtypeStruct((8, BLOCKS, 32, 128), bf16),
        in_specs=[pl.BlockSpec(memory_space=pltpu.HBM)] * 8,
        out_specs=pl.BlockSpec(memory_space=pl.ANY),
        scratch_shapes=[
            pltpu.SMEM(station_net.shape, jnp.int32),
            pltpu.SMEM(quality.shape, jnp.int32),
            pltpu.VMEM(traces.shape, f32),
            pltpu.VMEM(response_re.shape, f32),
            pltpu.VMEM(response_im.shape, f32),
            pltpu.VMEM(twiddle.shape, f32),
            pltpu.VMEM(outer.shape, f32),
            pltpu.VMEM((FFT, BLOCKS * 128), bf16),
            pltpu.VMEM((10, 8, 128), f32),
            pltpu.VMEM((128, 256), f32),
            pltpu.VMEM((128, 128), f32),
            pltpu.VMEM((128, 128), f32),
            pltpu.VMEM((2, 40, 128), f32),
            pltpu.VMEM((2, 40, 128), f32),
            pltpu.VMEM((2, 8, 16, 128), f32),
            pltpu.VMEM((8, 8, 128), jnp.int32),
            pltpu.VMEM((8, 16, 128), f32),
            pltpu.VMEM((8, 16, 128), f32),
            pltpu.VMEM((16, 1, 128), f32),
            pltpu.VMEM((2, 8, 1, 128), f32),
            pltpu.VMEM((16, 4, 16, 128), bf16),
            pltpu.VMEM((2, 8, 4, 16, 128), bf16),
            pltpu.VMEM((16, 4, 2, 16, 128), f32),
            pltpu.VMEM((16, 128), f32),
            pltpu.VMEM((16, 16, 128), f32),
            pltpu.VMEM((4096, 128), f32),
            pltpu.VMEM((256, FFT), bf16),
            pltpu.VMEM((8, BLOCKS, 32, 128), bf16),
            dma((7,)), dma, dma((2,)), dma((2,)), dma((8,)), dma((8,)), dma((8,)), dma((8,)),
            dma((3,)), dma((3,)), dma((8,)), dma((8,)), dma((16,)), dma((16,)), dma((8,)), dma((8,)),
            dma((16,)), dma((16,)), dma((8,)), dma((8,)), dma((2, 8)), dma((2, 8)),
        ],
        compiler_params=pltpu.CompilerParams(
            collective_id=0, has_side_effects=True, vmem_limit_bytes=64 << 20
        ),
    )(
        station_net, quality, traces, response_re, response_im,
        jnp.asarray(twiddle), jnp.asarray(outer), jnp.asarray(inverse),
    )
    return pl.pallas_call(
        place,
        out_shape=jax.ShapeDtypeStruct((2, 128, LAGS), f32),
        in_specs=[vmem],
        out_specs=vmem,
        scratch_shapes=[pltpu.VMEM((2 * BLOCKS * 128, 128), f32)],
        compiler_params=pltpu.CompilerParams(vmem_limit_bytes=16 << 20),
    )(lags)


def solution(mesh):
    return jax.shard_map(
        on_device,
        mesh=mesh,
        in_specs=(P("sta", "win"), P("sta", None), P("sta", None), P("sta"), P("sta", "win")),
        out_specs=P("sta", "win", None),
        check_vma=False,
    )
```

```python
import math

import jax
import jax.numpy as jnp
import ml_dtypes
import numpy as np
from jax import lax
from jax.experimental import pallas as pl
from jax.experimental.pallas import tpu as pltpu
from jax.sharding import PartitionSpec as P

MESH = pl.DeviceIdType.MESH
SEG, BINS, MAXLAG = 1200, 1024, 400
FFT = 2 * BINS
LAGS = 2 * MAXLAG + 1
BLOCKS = 7
CHUNKS = ((0, 2), (2, 2), (4, 2), (6, 1))
GROUPS = ((0, 4), (4, 3))
HIGHEST = lax.Precision.HIGHEST


def tables():
    f1 = np.arange(16)
    lane = np.arange(64)
    f2 = 8 * (lane % 8) + lane // 8
    r = np.arange(128)
    ang = 2 * np.pi * (f1[:, None] * r[None, :] % FFT) / FFT
    twiddle = np.stack([np.cos(ang), -np.sin(ang)]).astype(np.float32)
    ang = 2 * np.pi * (r[:, None] * f2[None, :] % 128) / 128
    c, s = np.cos(ang), np.sin(ang)
    outer = np.concatenate(
        [np.concatenate([c, -s], 1), np.concatenate([s, c], 1)], 0
    ).astype(np.float32)
    f = f1[:, None] + 16 * f2[None, :]
    k = np.arange(LAGS) - MAXLAG
    ang = 2 * np.pi * (f[:, :, None] * k % FFT) / FFT
    w = np.where(f == 0, 1.0, 2.0)[:, :, None] / math.sqrt(BINS)
    inverse = np.zeros((16, 128, BLOCKS * 128), np.float64)
    inverse[:, :64, :LAGS] = w * np.cos(ang)
    inverse[:, 64:, :LAGS] = -w * np.sin(ang)
    return twiddle, outer, inverse.reshape(FFT, BLOCKS * 128).astype(ml_dtypes.bfloat16)


def coords():
    s = lax.axis_index("sta")
    return s // 32, s // 4 % 8, s // 2 % 2, s % 2, lax.axis_index("win")


def device(y, z, xl, c, xh):
    return {"sta": ((y * 8 + z) * 2 + xl) * 2 + c, "win": xh}


def kernel(
    net_hbm, qual_hbm, tr_hbm, re_hbm, im_hbm, tw_hbm, outer_hbm, inv_hbm, out_ref,
    net_ref, qual_ref, tr_ref, tw_ref, outer_ref, inv,
    xs, lhs, xscr, sq, xsend, xrecv, gbuf, nbuf, csend, crecv, fa, fb, abuf, bbuf, rows, af, bf, qa, scale, mat, sbuf,
    isem, tsem, s_x, r_x, s_r1, r_r1, s_n, r_n, s_d, r_d, s_r2, r_r2, s_fa, r_fa, s_fb, r_fb, s_a, r_a, s_b, r_b,
    s_o, r_o,
):
    y, z, xl, c, xh = coords()
    me = y * 2 + xl
    own = y * 4 + xh * 2 + xl
    lane = lax.broadcasted_iota(jnp.int32, (16, 128), 1)
    low = lane < 64

    def swap(v):
        return pltpu.roll(v, 64, 1)

    def plane(p):
        return device(p // 2, z, p % 2, c, xh)

    def across(p):
        return device(p // 2, z, p % 2, c, 1 - xh)

    def moved(yy, st):
        return yy + (1 - 2 * (yy % 2)) * (1 - st) + (3 - 2 * yy) * st

    def which(yy, hh):
        return (yy // 2 + hh) % 2

    st_own = which(y, xh)
    home = moved(y, st_own)

    def slot_of(p):
        st = which(p // 2, xh)
        return (moved(p // 2, st) % 2) * 4 + p % 2 * 2 + st

    barrier = pltpu.get_barrier_semaphore()

    def greet(to):
        pl.semaphore_signal(barrier, inc=1, device_id=to, device_id_type=MESH)

    for d in range(1, 8):
        greet(device(y, (z + d) % 8, xl, c, xh))
        greet(plane((me + d) % 8))
    greet(device(y, z, xl, 1 - c, xh))
    greet(device(home, z, xl, c, 0))
    greet(device(home, z, xl, c, 1))

    sq[...] = jnp.zeros((128, 128), jnp.float32)
    loads = [
        pltpu.make_async_copy(src, dst, isem.at[i])
        for i, (src, dst) in enumerate(
            (
                (re_hbm, sq.at[pl.ds(0, 8)]), (im_hbm, sq.at[pl.ds(64, 8)]), (net_hbm, net_ref),
                (tr_hbm, tr_ref), (qual_hbm, qual_ref), (tw_hbm, tw_ref), (outer_hbm, outer_ref),
            )
        )
    ]
    for load in loads:
        load.start()
    table = pltpu.make_async_copy(inv_hbm, inv, tsem)
    table.start()

    for load in loads[:2]:
        load.wait()
    turned = sq[...].T
    resp = turned[0:16, :]
    for m in range(1, 8):
        resp = resp + pltpu.roll(turned[16 * m : 16 * m + 16, :], 8 * m, 1)
    square = resp * resp
    power = square + swap(square)
    level = 0.1 * (jnp.sum(square) / BINS) + 1e-06
    gbuf[c, z] = jnp.where(low, resp, -resp) / (power + level)
    loads[2].wait()
    row = lax.broadcasted_iota(jnp.int32, (8, 128), 0)
    nbuf[me] = jnp.where(row < 4, net_ref[0], net_ref[1])

    pl.semaphore_wait(barrier, 17)

    def remote(src, dst, ssem, rsem, to):
        return pltpu.make_async_remote_copy(
            src_ref=src, dst_ref=dst, send_sem=ssem, recv_sem=rsem, device_id=to,
            device_id_type=MESH,
        )

    sent = []

    def start(copy):
        copy.start()
        sent.append(copy)

    sibling = device(y, z, xl, 1 - c, xh)
    for d in (4, 3, 5, 2, 6, 1, 7):
        zz = (z + d) % 8
        start(
            remote(gbuf.at[c, z], gbuf.at[c, z], s_r1.at[zz], r_r1.at[z], device(y, zz, xl, c, xh))
        )
    for d in range(1, 8):
        p = (me + d) % 8
        start(remote(nbuf.at[me], nbuf.at[me], s_n.at[p], r_n.at[me], plane(p)))

    for load in loads[3:]:
        load.wait()

    for q in range(10):
        n = min(128, SEG - 128 * q)
        xs[q] = jnp.zeros((8, 128), jnp.float32)
        xs[q, 0:2, 0:n] = tr_ref[:, 128 * q : 128 * q + n]
        xs[q, 2:4, 0:n] = tr_ref[:, SEG + 128 * q : SEG + 128 * q + n]
    for f in range(9):
        parts = []
        for fn, sign in ((math.cos, 1.0), (math.sin, -1.0)):
            total = jnp.zeros((8, 128), jnp.float32)
            for q in range(10):
                w = sign * fn(2 * math.pi * (f * q % 16) / 16)
                if abs(w) > 1e-9:
                    total = total + (xs[q] if w == 1.0 else xs[q] * w)
            parts.append(total)
        for g in {f, (16 - f) % 16}:
            ar, ai = parts if g == f else (parts[0], -parts[1])
            tr, ti = tw_ref[0, g : g + 1, :], tw_ref[1, g : g + 1, :]
            lhs[8 * g : 8 * g + 8, 0:128] = ar * tr - ai * ti
            lhs[8 * g : 8 * g + 8, 128:256] = ar * ti + ai * tr
    xscr[...] = jnp.dot(
        lhs[...], outer_ref[...], precision=HIGHEST, preferred_element_type=jnp.float32
    )
    group = lax.broadcasted_iota(jnp.int32, (8, 128), 1) // 32
    for st in range(2):
        flags = jnp.zeros((8, 128), jnp.float32)
        for g in range(2):
            flag = qual_ref[st, g].astype(jnp.float32)
            xsend[st, 16 * g : 16 * g + 16] = xscr[pl.ds(2 * g + st, 16, stride=8), :] * flag
            flags = jnp.where(group == 2 * xh + g, flag, flags)
        xsend[st, 32:40] = flags

    for st in range(2):
        start(
            remote(xsend.at[st], xrecv.at[xh], s_x.at[st], r_x.at[xh],
                   device(moved(y, st), z, xl, c, y // 2))
        )
    for x in range(2):
        remote(xsend.at[0], xrecv.at[x], s_x.at[0], r_x.at[x], sibling).wait_recv()
    mark = xrecv[0, 32:33, :] + xrecv[1, 32:33, :]
    fa[own] = mark
    fb[c, z] = mark
    for d in range(1, 8):
        zz = (z + d) % 8
        remote(gbuf.at[c, zz], gbuf.at[c, zz], s_r1.at[zz], r_r1.at[zz], sibling).wait_recv()
    start(remote(gbuf.at[c], gbuf.at[c], s_d.at[0], r_d.at[0], sibling))
    for d in range(1, 8):
        zz = (z + d) % 8
        start(remote(fb.at[c, z], fb.at[c, z], s_fb.at[zz], r_fb.at[z], device(y, zz, xl, c, xh)))
    for d in range(1, 8):
        p = (me + d) % 8
        remote(nbuf.at[p], nbuf.at[p], s_n.at[p], r_n.at[p], plane(p)).wait_recv()
    remote(gbuf.at[1 - c], gbuf.at[1 - c], s_d.at[0], r_d.at[0], sibling).wait_recv()

    base = y * 32 + xl * 2

    def choose(p):
        st = which(p // 2, xh)
        want = nbuf[moved(p // 2, st) * 2 + p % 2, pl.ds(4 * st, 1), :]
        acc = jnp.zeros((16, 128), jnp.float32)
        for cc in range(2):
            for zz in range(8):
                acc = jnp.where(want == base + 4 * zz + cc, gbuf[cc, zz], acc)
        return acc

    for d in (4, 5, 3, 2, 6, 1, 7):
        p = (me + d) % 8
        csend[p] = choose(p)
        start(remote(csend.at[p], crecv.at[me], s_r2.at[p], r_r2.at[me], plane(p)))
    factor = choose(me)
    specs = [xrecv[x, 16 * g : 16 * g + 16, :] for x in range(2) for g in range(2)]
    crossed = [swap(spec) for spec in specs]
    for d in range(1, 8):
        p = (me + d) % 8
        remote(csend.at[p], crecv.at[p], s_r2.at[p], r_r2.at[p], plane(p)).wait_recv()
        factor = factor + crecv[p]

    turn = swap(factor)
    f_re = jnp.where(low, factor, turn)
    f_im = jnp.where(low, -turn, factor)
    for s in range(4):
        dec = specs[s] * f_re + crossed[s] * f_im
        square = dec * dec
        energy = square + swap(square)
        mean = jnp.sum(square) / BINS + 1e-06
        abuf[own, s] = (dec / jnp.sqrt(energy + 0.5 * mean)).astype(jnp.bfloat16)

    for d in (4, 3, 5, 2, 6, 1, 7):
        zz = (z + d) % 8
        start(
            remote(abuf.at[own], bbuf.at[c, z], s_b.at[zz], r_b.at[z], device(y, zz, xl, c, xh))
        )
    for d in (4, 5, 3, 2, 6, 1, 7, 0):
        p = (me + d) % 8
        if d > 0:
            start(
                remote(abuf.at[own], abuf.at[own], s_a.at[p // 2 * 4 + xh * 2 + p % 2], r_a.at[own],
                       plane(p))
            )
        start(
            remote(abuf.at[own], abuf.at[own], s_a.at[p // 2 * 4 + (1 - xh) * 2 + p % 2],
                   r_a.at[own], across(p))
        )
    bbuf[c, z] = abuf[own]

    for d in range(8):
        p = (me + d) % 8
        if d > 0:
            start(
                remote(fa.at[own], fa.at[own], s_fa.at[p // 2 * 4 + xh * 2 + p % 2], r_fa.at[own],
                       plane(p))
            )
        start(
            remote(fa.at[own], fa.at[own], s_fa.at[p // 2 * 4 + (1 - xh) * 2 + p % 2], r_fa.at[own],
                   across(p))
        )
    for d in range(1, 8):
        zz = (z + d) % 8
        remote(fb.at[c, z], fb.at[c, zz], s_fb.at[zz], r_fb.at[zz], sibling).wait_recv()
    start(remote(fb.at[c], fb.at[c], s_d.at[1], r_d.at[1], sibling))

    for d in range(1, 8):
        zz = (z + d) % 8
        remote(abuf.at[own], bbuf.at[c, zz], s_b.at[zz], r_b.at[zz], sibling).wait_recv()
    start(remote(bbuf.at[c], bbuf.at[c], s_d.at[2], r_d.at[2], sibling))
    for d in range(1, 16):
        s = (own + d) % 16
        remote(fa.at[own], fa.at[s], s_fa.at[s], r_fa.at[s], sibling).wait_recv()
    remote(fb.at[1 - c], fb.at[1 - c], s_d.at[1], r_d.at[1], sibling).wait_recv()

    def first_slot(i, st):
        p = (me + i + 3) % 8
        return moved(p // 2, st) * 4 + p // 4 * 2 + p % 2

    for cc in range(2):
        for zz in range(8):
            qa[8 * cc + zz : 8 * cc + zz + 1, :] = fb[cc, zz]
    for i in range(8):
        for st in range(2):
            count = qa[...] * fa[first_slot(i, st)]
            count = count + swap(count)
            count = count + pltpu.roll(count, 32, 1)
            scale[2 * i + st] = 1.0 / jnp.maximum(count, 1.0)

    for d in range(1, 16):
        s = (own + d) % 16
        remote(abuf.at[own], abuf.at[s], s_a.at[s], r_a.at[s], sibling).wait_recv()

    def first(i, _):
        for st in range(2):
            slot = first_slot(i, st)
            for s in range(4):
                v = abuf[slot, s].astype(jnp.float32)
                t = swap(v)
                af[2 * i + st, s, 0] = jnp.where(low, v, -t)
                af[2 * i + st, s, 1] = jnp.where(low, t, v)
        return 0

    lax.fori_loop(0, 8, first, 0)
    remote(bbuf.at[1 - c], bbuf.at[1 - c], s_d.at[2], r_d.at[2], sibling).wait_recv()

    for b in range(16):
        for s in range(4):
            rows[s, 16 * b : 16 * b + 16, :] = bbuf[b // 8, b % 8, s].astype(jnp.float32)
    for s in range(4):
        for f in range(16):
            v = rows[s, pl.ds(f, 16, stride=16), :]
            bf[f, s, 0] = v
            bf[f, s, 1] = swap(v)

    mine = slot_of(me)
    for part in range(2):

        def pairs(f, _, part=part):
            other = [(bf[f, s, 0], bf[f, s, 1]) for s in range(4)]
            at = pl.multiple_of(128 * f, 128)
            for a in range(8 * part, 8 * part + 8):
                acc = None
                for s in range(4):
                    term = af[a, s, 0, pl.ds(f, 1), :] * other[s][0]
                    term = term + af[a, s, 1, pl.ds(f, 1), :] * other[s][1]
                    acc = term if acc is None else acc + term
                mat[16 * a : 16 * a + 16, pl.ds(at, 128)] = (acc * scale[a]).astype(jnp.bfloat16)
            return 0

        lax.fori_loop(0, 16, pairs, 0)
        if part == 0:
            table.wait()
        for n, count in CHUNKS:
            lags = jnp.dot(
                mat[128 * part : 128 * part + 128, :],
                inv[:, 128 * n : 128 * (n + count)],
                preferred_element_type=jnp.float32,
            ).astype(jnp.bfloat16)
            for i in range(4):
                for j in range(count):
                    sbuf[4 * part + i, n + j] = lags[
                        32 * i : 32 * i + 32, 128 * j : 128 * j + 128
                    ]
            for k, (at, many) in enumerate(GROUPS):
                if n + count == at + many:
                    for i in range(4 * part, 4 * part + 4):
                        if i != 5:
                            start(
                                remote(sbuf.at[i, pl.ds(at, many)], out_ref.at[mine, pl.ds(at, many)],
                                       s_o.at[k, i], r_o.at[k, mine], plane((me + i + 3) % 8))
                            )
    keep = pltpu.make_async_copy(sbuf.at[5], out_ref.at[mine], tsem)
    keep.start()
    for k, (at, many) in enumerate(GROUPS):
        for d in range(1, 8):
            s = slot_of((me + d) % 8)
            remote(sbuf.at[0, pl.ds(at, many)], out_ref.at[s, pl.ds(at, many)],
                   s_o.at[k, 0], r_o.at[k, s], sibling).wait_recv()
    keep.wait()
    for copy in sent:
        copy.wait_send()


def place(lags_ref, out_ref, rows, stage, sem):
    copies = []
    for n in range(BLOCKS):
        width = min(128, LAGS - 128 * n)
        for a in range(2):
            for s in range(8):
                for st in range(2):
                    at = s // 4 * 64 + s // 2 % 2 * 4 + s % 2 + st * 2
                    v = lags_ref[s, n, 16 * a + 8 * st : 16 * a + 8 * st + 8, :]
                    rows[2 * n + a, pl.ds(at, 8, stride=8), :] = v.astype(jnp.float32)
            stage[128 * n : 128 * n + 128, a, :] = rows[2 * n + a].T
        part = pl.ds(128 * n, width)
        copies.append(pltpu.make_async_copy(stage.at[part], out_ref.at[part], sem.at[n]))
        copies[-1].start()
    for copy in copies:
        copy.wait()


def on_device(traces, response_re, response_im, station_net, quality):
    twiddle, outer, inverse = tables()
    f32, bf16 = jnp.float32, jnp.bfloat16
    vmem = pl.BlockSpec(memory_space=pltpu.VMEM)
    dma = pltpu.SemaphoreType.DMA
    lags = pl.pallas_call(
        kernel,
        out_shape=jax.ShapeDtypeStruct((8, BLOCKS, 32, 128), bf16),
        in_specs=[pl.BlockSpec(memory_space=pltpu.HBM)] * 8,
        out_specs=pl.BlockSpec(memory_space=pl.ANY),
        scratch_shapes=[
            pltpu.SMEM(station_net.shape, jnp.int32),
            pltpu.SMEM(quality.shape, jnp.int32),
            pltpu.VMEM(traces.shape, f32),
            pltpu.VMEM(twiddle.shape, f32),
            pltpu.VMEM(outer.shape, f32),
            pltpu.VMEM((FFT, BLOCKS * 128), bf16),
            pltpu.VMEM((10, 8, 128), f32),
            pltpu.VMEM((128, 256), f32),
            pltpu.VMEM((128, 128), f32),
            pltpu.VMEM((128, 128), f32),
            pltpu.VMEM((2, 40, 128), f32),
            pltpu.VMEM((2, 40, 128), f32),
            pltpu.VMEM((2, 8, 16, 128), f32),
            pltpu.VMEM((8, 8, 128), jnp.int32),
            pltpu.VMEM((8, 16, 128), f32),
            pltpu.VMEM((8, 16, 128), f32),
            pltpu.VMEM((16, 1, 128), f32),
            pltpu.VMEM((2, 8, 1, 128), f32),
            pltpu.VMEM((16, 4, 16, 128), bf16),
            pltpu.VMEM((2, 8, 4, 16, 128), bf16),
            pltpu.VMEM((4, 256, 128), f32),
            pltpu.VMEM((16, 4, 2, 16, 128), f32),
            pltpu.VMEM((16, 4, 2, 16, 128), f32),
            pltpu.VMEM((16, 128), f32),
            pltpu.VMEM((16, 16, 128), f32),
            pltpu.VMEM((256, FFT), bf16),
            pltpu.VMEM((8, BLOCKS, 32, 128), bf16),
            dma((7,)), dma, dma((2,)), dma((2,)), dma((8,)), dma((8,)), dma((8,)), dma((8,)),
            dma((3,)), dma((3,)), dma((8,)), dma((8,)), dma((16,)), dma((16,)), dma((8,)), dma((8,)),
            dma((16,)), dma((16,)), dma((8,)), dma((8,)), dma((2, 8)), dma((2, 8)),
        ],
        compiler_params=pltpu.CompilerParams(
            collective_id=0, has_side_effects=True, vmem_limit_bytes=40 << 20
        ),
    )(
        *(
            pltpu.with_memory_space_constraint(v, pltpu.HBM)
            for v in (
                station_net, quality, traces, response_re.reshape(8, 128),
                response_im.reshape(8, 128), jnp.asarray(twiddle), jnp.asarray(outer),
                jnp.asarray(inverse),
            )
        )
    )
    placed = pl.pallas_call(
        place,
        out_shape=jax.ShapeDtypeStruct((LAGS, 2, 128), f32),
        in_specs=[vmem],
        out_specs=pl.BlockSpec(memory_space=pl.ANY),
        scratch_shapes=[
            pltpu.VMEM((2 * BLOCKS, 128, 128), f32),
            pltpu.VMEM((128 * BLOCKS, 2, 128), f32),
            dma((BLOCKS,)),
        ],
        compiler_params=pltpu.CompilerParams(vmem_limit_bytes=16 << 20),
    )(lags)
    return placed.transpose(1, 2, 0)


def solution(mesh):
    return jax.shard_map(
        on_device,
        mesh=mesh,
        in_specs=(P("sta", "win"), P("sta", None), P("sta", None), P("sta"), P("sta", "win")),
        out_specs=P("sta", "win", None),
        check_vma=False,
    )
```

```python
import math

import jax
import jax.numpy as jnp
import ml_dtypes
import numpy as np
from jax import lax
from jax.experimental import pallas as pl
from jax.experimental.pallas import tpu as pltpu
from jax.sharding import PartitionSpec as P

MESH = pl.DeviceIdType.MESH
SEG, BINS, MAXLAG = 1200, 1024, 400
FFT = 2 * BINS
LAGS = 2 * MAXLAG + 1
BLOCKS = 7
CHUNKS = ((0, 2), (2, 2), (4, 2), (6, 1))
GROUPS = ((0, 4), (4, 2), (6, 1))
PARTS = ((0, 4), (4, 8))
HIGHEST = lax.Precision.HIGHEST


def tables():
    f1 = np.arange(16)
    lane = np.arange(64)
    f2 = 8 * (lane % 8) + lane // 8
    r = np.arange(128)
    ang = 2 * np.pi * (f1[:, None] * r[None, :] % FFT) / FFT
    twiddle = np.stack([np.cos(ang), -np.sin(ang)]).astype(np.float32)
    ang = 2 * np.pi * (r[:, None] * f2[None, :] % 128) / 128
    c, s = np.cos(ang), np.sin(ang)
    outer = np.concatenate(
        [np.concatenate([c, -s], 1), np.concatenate([s, c], 1)], 0
    ).astype(np.float32)
    f = f1[:, None] + 16 * f2[None, :]
    k = np.arange(LAGS) - MAXLAG
    ang = 2 * np.pi * (f[:, :, None] * k % FFT) / FFT
    w = np.where(f == 0, 1.0, 2.0)[:, :, None] / math.sqrt(BINS)
    inverse = np.zeros((16, 128, BLOCKS * 128), np.float64)
    inverse[:, :64, :LAGS] = w * np.cos(ang)
    inverse[:, 64:, :LAGS] = -w * np.sin(ang)
    return twiddle, outer, inverse.reshape(FFT, BLOCKS * 128).astype(ml_dtypes.bfloat16)


def coords():
    s = lax.axis_index("sta")
    return s // 32, s // 4 % 8, s // 2 % 2, s % 2, lax.axis_index("win")


def device(y, z, xl, c, xh):
    return {"sta": ((y * 8 + z) * 2 + xl) * 2 + c, "win": xh}


def kernel(
    net_hbm, qual_hbm, tr_hbm, re_hbm, im_hbm, tw_hbm, outer_hbm, inv_hbm, out_ref,
    net_ref, qual_ref, tr_ref, tw_ref, outer_ref, inv,
    xs, lhs, xscr, sq, xsend, xrecv, gbuf, nbuf, csend, crecv, fa, fb, abuf, bbuf, rows, af, bf, qa, scale, mat, sbuf, rbuf, turn_buf,
    isem, tsem, s_x, r_x, s_r1, r_r1, s_n, r_n, s_d, r_d, s_r2, r_r2, s_fa, r_fa, s_fb, r_fb, s_a, r_a, s_b, r_b,
    s_o, r_o,
):
    y, z, xl, c, xh = coords()
    me = y * 2 + xl
    own = y * 4 + xh * 2 + xl
    lane = lax.broadcasted_iota(jnp.int32, (16, 128), 1)
    low = lane < 64

    def swap(v):
        return pltpu.roll(v, 64, 1)

    def plane(p):
        return device(p // 2, z, p % 2, c, xh)

    def across(p):
        return device(p // 2, z, p % 2, c, 1 - xh)

    def moved(yy, st):
        return yy + (1 - 2 * (yy % 2)) * (1 - st) + (3 - 2 * yy) * st

    def which(yy, hh):
        return (yy // 2 + hh) % 2

    st_own = which(y, xh)
    home = moved(y, st_own)

    def slot_of(p):
        st = which(p // 2, xh)
        return (moved(p // 2, st) % 2) * 4 + p % 2 * 2 + st

    barrier = pltpu.get_barrier_semaphore()

    def greet(to):
        pl.semaphore_signal(barrier, inc=1, device_id=to, device_id_type=MESH)

    for d in range(1, 8):
        greet(device(y, (z + d) % 8, xl, c, xh))
        greet(plane((me + d) % 8))
    greet(device(y, z, xl, 1 - c, xh))
    greet(device(home, z, xl, c, 0))
    greet(device(home, z, xl, c, 1))

    sq[...] = jnp.zeros((128, 128), jnp.float32)
    loads = [
        pltpu.make_async_copy(src, dst, isem.at[i])
        for i, (src, dst) in enumerate(
            (
                (re_hbm, sq.at[pl.ds(0, 8)]), (im_hbm, sq.at[pl.ds(64, 8)]), (net_hbm, net_ref),
                (tr_hbm, tr_ref), (qual_hbm, qual_ref), (tw_hbm, tw_ref), (outer_hbm, outer_ref),
            )
        )
    ]
    for load in loads:
        load.start()
    table = pltpu.make_async_copy(inv_hbm, inv, tsem)
    table.start()

    for load in loads[:2]:
        load.wait()
    turned = sq[...].T
    resp = turned[0:16, :]
    for m in range(1, 8):
        resp = resp + pltpu.roll(turned[16 * m : 16 * m + 16, :], 8 * m, 1)
    square = resp * resp
    power = square + swap(square)
    level = 0.1 * (jnp.sum(square) / BINS) + 1e-06
    gbuf[c, z] = jnp.where(low, resp, -resp) / (power + level)
    loads[2].wait()
    row = lax.broadcasted_iota(jnp.int32, (8, 128), 0)
    nbuf[me] = jnp.where(row < 4, net_ref[0], net_ref[1])

    pl.semaphore_wait(barrier, 17)

    def remote(src, dst, ssem, rsem, to):
        return pltpu.make_async_remote_copy(
            src_ref=src, dst_ref=dst, send_sem=ssem, recv_sem=rsem, device_id=to,
            device_id_type=MESH,
        )

    sent = []

    def start(copy):
        copy.start()
        sent.append(copy)

    sibling = device(y, z, xl, 1 - c, xh)
    for d in (4, 3, 5, 2, 6, 1, 7):
        zz = (z + d) % 8
        start(
            remote(gbuf.at[c, z], gbuf.at[c, z], s_r1.at[zz], r_r1.at[z], device(y, zz, xl, c, xh))
        )
    for d in range(1, 8):
        p = (me + d) % 8
        start(remote(nbuf.at[me], nbuf.at[me], s_n.at[p], r_n.at[me], plane(p)))

    for load in loads[3:]:
        load.wait()

    for q in range(10):
        n = min(128, SEG - 128 * q)
        xs[q] = jnp.zeros((8, 128), jnp.float32)
        xs[q, 0:2, 0:n] = tr_ref[:, 128 * q : 128 * q + n]
        xs[q, 2:4, 0:n] = tr_ref[:, SEG + 128 * q : SEG + 128 * q + n]
    for f in range(9):
        parts = []
        for fn, sign in ((math.cos, 1.0), (math.sin, -1.0)):
            total = jnp.zeros((8, 128), jnp.float32)
            for q in range(10):
                w = sign * fn(2 * math.pi * (f * q % 16) / 16)
                if abs(w) > 1e-9:
                    total = total + (xs[q] if w == 1.0 else xs[q] * w)
            parts.append(total)
        for g in {f, (16 - f) % 16}:
            ar, ai = parts if g == f else (parts[0], -parts[1])
            tr, ti = tw_ref[0, g : g + 1, :], tw_ref[1, g : g + 1, :]
            lhs[8 * g : 8 * g + 8, 0:128] = ar * tr - ai * ti
            lhs[8 * g : 8 * g + 8, 128:256] = ar * ti + ai * tr
    xscr[...] = jnp.dot(
        lhs[...], outer_ref[...], precision=HIGHEST, preferred_element_type=jnp.float32
    )
    group = lax.broadcasted_iota(jnp.int32, (8, 128), 1) // 32
    for st in range(2):
        flags = jnp.zeros((8, 128), jnp.float32)
        for g in range(2):
            flag = qual_ref[st, g].astype(jnp.float32)
            xsend[st, 16 * g : 16 * g + 16] = xscr[pl.ds(2 * g + st, 16, stride=8), :] * flag
            flags = jnp.where(group == 2 * xh + g, flag, flags)
        xsend[st, 32:40] = flags

    for st in range(2):
        start(
            remote(xsend.at[st], xrecv.at[xh], s_x.at[st], r_x.at[xh],
                   device(moved(y, st), z, xl, c, y // 2))
        )
    for x in range(2):
        remote(xsend.at[0], xrecv.at[x], s_x.at[0], r_x.at[x], sibling).wait_recv()
    mark = xrecv[0, 32:33, :] + xrecv[1, 32:33, :]
    fa[own] = mark
    fb[c, z] = mark
    for d in range(1, 8):
        zz = (z + d) % 8
        remote(gbuf.at[c, zz], gbuf.at[c, zz], s_r1.at[zz], r_r1.at[zz], sibling).wait_recv()
    start(remote(gbuf.at[c], gbuf.at[c], s_d.at[0], r_d.at[0], sibling))
    for d in range(1, 8):
        zz = (z + d) % 8
        start(remote(fb.at[c, z], fb.at[c, z], s_fb.at[zz], r_fb.at[z], device(y, zz, xl, c, xh)))
    for d in range(1, 8):
        p = (me + d) % 8
        remote(nbuf.at[p], nbuf.at[p], s_n.at[p], r_n.at[p], plane(p)).wait_recv()
    remote(gbuf.at[1 - c], gbuf.at[1 - c], s_d.at[0], r_d.at[0], sibling).wait_recv()

    base = y * 32 + xl * 2

    def choose(p):
        st = which(p // 2, xh)
        want = nbuf[moved(p // 2, st) * 2 + p % 2, pl.ds(4 * st, 1), :]
        acc = jnp.zeros((16, 128), jnp.float32)
        for cc in range(2):
            for zz in range(8):
                acc = jnp.where(want == base + 4 * zz + cc, gbuf[cc, zz], acc)
        return acc

    for d in (4, 5, 3, 2, 6, 1, 7):
        p = (me + d) % 8
        csend[p] = choose(p)
        start(remote(csend.at[p], crecv.at[me], s_r2.at[p], r_r2.at[me], plane(p)))
    factor = choose(me)
    specs = [xrecv[x, 16 * g : 16 * g + 16, :] for x in range(2) for g in range(2)]
    crossed = [swap(spec) for spec in specs]
    for d in range(1, 8):
        p = (me + d) % 8
        remote(csend.at[p], crecv.at[p], s_r2.at[p], r_r2.at[p], plane(p)).wait_recv()
        factor = factor + crecv[p]

    turn = swap(factor)
    f_re = jnp.where(low, factor, turn)
    f_im = jnp.where(low, -turn, factor)
    for s in range(4):
        dec = specs[s] * f_re + crossed[s] * f_im
        square = dec * dec
        energy = square + swap(square)
        mean = jnp.sum(square) / BINS + 1e-06
        abuf[own, s] = (dec / jnp.sqrt(energy + 0.5 * mean)).astype(jnp.bfloat16)

    for d in (4, 3, 5, 2, 6, 1, 7):
        zz = (z + d) % 8
        start(
            remote(abuf.at[own], bbuf.at[c, z], s_b.at[zz], r_b.at[z], device(y, zz, xl, c, xh))
        )
    for d in (4, 5, 3, 2, 6, 1, 7, 0):
        p = (me + d) % 8
        if d > 0:
            start(
                remote(abuf.at[own], abuf.at[own], s_a.at[p // 2 * 4 + xh * 2 + p % 2], r_a.at[own],
                       plane(p))
            )
        start(
            remote(abuf.at[own], abuf.at[own], s_a.at[p // 2 * 4 + (1 - xh) * 2 + p % 2],
                   r_a.at[own], across(p))
        )
    bbuf[c, z] = abuf[own]

    for d in range(8):
        p = (me + d) % 8
        if d > 0:
            start(
                remote(fa.at[own], fa.at[own], s_fa.at[p // 2 * 4 + xh * 2 + p % 2], r_fa.at[own],
                       plane(p))
            )
        start(
            remote(fa.at[own], fa.at[own], s_fa.at[p // 2 * 4 + (1 - xh) * 2 + p % 2], r_fa.at[own],
                   across(p))
        )
    for d in range(1, 8):
        zz = (z + d) % 8
        remote(fb.at[c, z], fb.at[c, zz], s_fb.at[zz], r_fb.at[zz], sibling).wait_recv()
    start(remote(fb.at[c], fb.at[c], s_d.at[1], r_d.at[1], sibling))

    for d in range(1, 8):
        zz = (z + d) % 8
        remote(abuf.at[own], bbuf.at[c, zz], s_b.at[zz], r_b.at[zz], sibling).wait_recv()
    start(remote(bbuf.at[c], bbuf.at[c], s_d.at[2], r_d.at[2], sibling))
    for d in range(1, 16):
        s = (own + d) % 16
        remote(fa.at[own], fa.at[s], s_fa.at[s], r_fa.at[s], sibling).wait_recv()
    remote(fb.at[1 - c], fb.at[1 - c], s_d.at[1], r_d.at[1], sibling).wait_recv()

    def first_slot(i, st):
        p = (me + i + 3) % 8
        return moved(p // 2, st) * 4 + p // 4 * 2 + p % 2

    for cc in range(2):
        for zz in range(8):
            qa[8 * cc + zz : 8 * cc + zz + 1, :] = fb[cc, zz]
    for i in range(8):
        for st in range(2):
            count = qa[...] * fa[first_slot(i, st)]
            count = count + swap(count)
            count = count + pltpu.roll(count, 32, 1)
            scale[2 * i + st] = 1.0 / jnp.maximum(count, 1.0)

    for d in range(1, 16):
        s = (own + d) % 16
        remote(abuf.at[own], abuf.at[s], s_a.at[s], r_a.at[s], sibling).wait_recv()

    def first(i, _):
        for st in range(2):
            slot = first_slot(i, st)
            for s in range(4):
                v = abuf[slot, s].astype(jnp.float32)
                t = swap(v)
                af[2 * i + st, s, 0] = jnp.where(low, v, -t)
                af[2 * i + st, s, 1] = jnp.where(low, t, v)
        return 0

    lax.fori_loop(0, 8, first, 0)
    remote(bbuf.at[1 - c], bbuf.at[1 - c], s_d.at[2], r_d.at[2], sibling).wait_recv()

    for b in range(16):
        for s in range(4):
            rows[s, 16 * b : 16 * b + 16, :] = bbuf[b // 8, b % 8, s].astype(jnp.float32)
    for s in range(4):
        for f in range(16):
            v = rows[s, pl.ds(f, 16, stride=16), :]
            bf[f, s, 0] = v
            bf[f, s, 1] = swap(v)

    mine = slot_of(me)
    for lo, hi in PARTS:

        def pairs(f, _, lo=lo, hi=hi):
            other = [(bf[f, s, 0], bf[f, s, 1]) for s in range(4)]
            at = pl.multiple_of(128 * f, 128)
            for a in range(2 * lo, 2 * hi):
                acc = None
                for s in range(4):
                    term = af[a, s, 0, pl.ds(f, 1), :] * other[s][0]
                    term = term + af[a, s, 1, pl.ds(f, 1), :] * other[s][1]
                    acc = term if acc is None else acc + term
                mat[16 * a : 16 * a + 16, pl.ds(at, 128)] = (acc * scale[a]).astype(jnp.bfloat16)
            return 0

        lax.fori_loop(0, 16, pairs, 0)
        if lo == 0:
            table.wait()
        for n, count in CHUNKS:
            lags = jnp.dot(
                mat[32 * lo : 32 * hi, :],
                inv[:, 128 * n : 128 * (n + count)],
                preferred_element_type=jnp.float32,
            ).astype(jnp.bfloat16)
            for i in range(hi - lo):
                for j in range(count):
                    sbuf[lo + i, n + j] = lags[32 * i : 32 * i + 32, 128 * j : 128 * j + 128]
            for k, (at, many) in enumerate(GROUPS):
                if n + count == at + many:
                    for i in range(lo, hi):
                        if i != 5:
                            start(
                                remote(sbuf.at[i, pl.ds(at, many)], rbuf.at[mine, pl.ds(at, many)],
                                       s_o.at[k, i], r_o.at[k, mine], plane((me + i + 3) % 8))
                            )
    keep = pltpu.make_async_copy(sbuf.at[5], rbuf.at[mine], tsem)
    keep.start()
    keep.wait()
    for k, (at, many) in enumerate(GROUPS):
        for d in range(1, 8):
            s = slot_of((me + d) % 8)
            remote(sbuf.at[0, pl.ds(at, many)], rbuf.at[s, pl.ds(at, many)],
                   s_o.at[k, 0], r_o.at[k, s], sibling).wait_recv()
        for n in range(at, at + many):
            width = min(128, LAGS - 128 * n)
            for a in range(2):
                for s in range(8):
                    for st in range(2):
                        to = s // 4 * 64 + s // 2 % 2 * 4 + s % 2 + st * 2
                        v = rbuf[s, n, 16 * a + 8 * st : 16 * a + 8 * st + 8, :]
                        turn_buf[2 * n + a, pl.ds(to, 8, stride=8), :] = v.astype(jnp.float32)
                out_ref[128 * n : 128 * n + width, a, :] = turn_buf[2 * n + a].T[:width]
    for copy in sent:
        copy.wait_send()


def on_device(traces, response_re, response_im, station_net, quality):
    twiddle, outer, inverse = tables()
    f32, bf16 = jnp.float32, jnp.bfloat16
    dma = pltpu.SemaphoreType.DMA
    lags = pl.pallas_call(
        kernel,
        out_shape=jax.ShapeDtypeStruct((LAGS, 2, 128), f32),
        in_specs=[pl.BlockSpec(memory_space=pltpu.HBM)] * 8,
        out_specs=pl.BlockSpec(memory_space=pltpu.VMEM),
        scratch_shapes=[
            pltpu.SMEM(station_net.shape, jnp.int32),
            pltpu.SMEM(quality.shape, jnp.int32),
            pltpu.VMEM(traces.shape, f32),
            pltpu.VMEM(twiddle.shape, f32),
            pltpu.VMEM(outer.shape, f32),
            pltpu.VMEM((FFT, BLOCKS * 128), bf16),
            pltpu.VMEM((10, 8, 128), f32),
            pltpu.VMEM((128, 256), f32),
            pltpu.VMEM((128, 128), f32),
            pltpu.VMEM((128, 128), f32),
            pltpu.VMEM((2, 40, 128), f32),
            pltpu.VMEM((2, 40, 128), f32),
            pltpu.VMEM((2, 8, 16, 128), f32),
            pltpu.VMEM((8, 8, 128), jnp.int32),
            pltpu.VMEM((8, 16, 128), f32),
            pltpu.VMEM((8, 16, 128), f32),
            pltpu.VMEM((16, 1, 128), f32),
            pltpu.VMEM((2, 8, 1, 128), f32),
            pltpu.VMEM((16, 4, 16, 128), bf16),
            pltpu.VMEM((2, 8, 4, 16, 128), bf16),
            pltpu.VMEM((4, 256, 128), f32),
            pltpu.VMEM((16, 4, 2, 16, 128), f32),
            pltpu.VMEM((16, 4, 2, 16, 128), f32),
            pltpu.VMEM((16, 128), f32),
            pltpu.VMEM((16, 16, 128), f32),
            pltpu.VMEM((256, FFT), bf16),
            pltpu.VMEM((8, BLOCKS, 32, 128), bf16),
            pltpu.VMEM((8, BLOCKS, 32, 128), bf16),
            pltpu.VMEM((2 * BLOCKS, 128, 128), f32),
            dma((7,)), dma, dma((2,)), dma((2,)), dma((8,)), dma((8,)), dma((8,)), dma((8,)),
            dma((3,)), dma((3,)), dma((8,)), dma((8,)), dma((16,)), dma((16,)), dma((8,)), dma((8,)),
            dma((16,)), dma((16,)), dma((8,)), dma((8,)), dma((4, 8)), dma((4, 8)),
        ],
        compiler_params=pltpu.CompilerParams(
            collective_id=0, has_side_effects=True, vmem_limit_bytes=40 << 20
        ),
    )(
        *(
            pltpu.with_memory_space_constraint(v, pltpu.HBM)
            for v in (
                station_net, quality, traces, response_re.reshape(8, 128),
                response_im.reshape(8, 128), jnp.asarray(twiddle), jnp.asarray(outer),
                jnp.asarray(inverse),
            )
        )
    )
    return lags.transpose(1, 2, 0)


def solution(mesh):
    return jax.shard_map(
        on_device,
        mesh=mesh,
        in_specs=(P("sta", "win"), P("sta", None), P("sta", None), P("sta"), P("sta", "win")),
        out_specs=P("sta", "win", None),
        check_vma=False,
    )
```

```python
import math

import jax
import jax.numpy as jnp
import ml_dtypes
import numpy as np
from jax import lax
from jax.experimental import pallas as pl
from jax.experimental.pallas import tpu as pltpu
from jax.sharding import PartitionSpec as P

MESH = pl.DeviceIdType.MESH
SEG, BINS, MAXLAG = 1200, 1024, 400
FFT = 2 * BINS
LAGS = 2 * MAXLAG + 1
ROWS = 208
CHUNKS = ((0, 0, 128), (256, 128, 80))
PARTS = ((0, 2), (2, 4), (4, 6), (6, 8))
HIGHEST = lax.Precision.HIGHEST


def tables():
    f1 = np.arange(16)
    lane = np.arange(64)
    f2 = 8 * (lane % 8) + lane // 8
    r = np.arange(128)
    ang = 2 * np.pi * (f1[:, None] * r[None, :] % FFT) / FFT
    twiddle = np.stack([np.cos(ang), -np.sin(ang)]).astype(np.float32)
    ang = 2 * np.pi * (r[:, None] * f2[None, :] % 128) / 128
    c, s = np.cos(ang), np.sin(ang)
    outer = np.concatenate(
        [np.concatenate([c, -s], 1), np.concatenate([s, c], 1)], 0
    ).astype(np.float32)
    f = np.concatenate([f1[:8, None] + 16 * f2, f1[8:, None] + 16 * f2], 1).reshape(BINS)
    k = np.concatenate([np.arange(384), np.tile(384 + np.arange(32), 4)])
    ang = 2 * np.pi * (f[:, None] * k % FFT) / FFT
    w = np.where(f == 0, 1.0, 2.0)[:, None] / math.sqrt(BINS)
    inverse = np.stack([w * np.cos(ang), w * np.sin(ang)]).astype(ml_dtypes.bfloat16)
    return twiddle, outer, inverse


def coords():
    s = lax.axis_index("sta")
    return s // 32, s // 4 % 8, s // 2 % 2, s % 2, lax.axis_index("win")


def device(y, z, xl, c, xh):
    return {"sta": ((y * 8 + z) * 2 + xl) * 2 + c, "win": xh}


def kernel(
    net_hbm, qual_hbm, tr_hbm, re_hbm, im_hbm, tw_hbm, outer_hbm, inv_hbm, out_ref,
    net_ref, qual_ref, tr_ref, tw_ref, outer_ref, inv,
    xs, lhs, xscr, sq, xsend, xrecv, gbuf, nbuf, csend, crecv, fa, fb, abuf, bbuf, rows, af, bf, qa, scale, mat, sbuf, rbuf, turn_buf,
    isem, tsem, s_x, r_x, s_r1, r_r1, s_n, r_n, s_d, r_d, s_r2, r_r2, s_fa, r_fa, s_fb, r_fb, s_a, r_a, s_b, r_b,
    s_o, r_o,
):
    y, z, xl, c, xh = coords()
    me = y * 2 + xl
    own = y * 4 + xh * 2 + xl
    lane = lax.broadcasted_iota(jnp.int32, (16, 128), 1)
    low = lane < 64

    def swap(v):
        return pltpu.roll(v, 64, 1)

    def plane(p):
        return device(p // 2, z, p % 2, c, xh)

    def across(p):
        return device(p // 2, z, p % 2, c, 1 - xh)

    def moved(yy, st):
        return yy + (1 - 2 * (yy % 2)) * (1 - st) + (3 - 2 * yy) * st

    def which(yy, hh):
        return (yy // 2 + hh) % 2

    st_own = which(y, xh)
    home = moved(y, st_own)

    def slot_of(p):
        st = which(p // 2, xh)
        return (moved(p // 2, st) % 2) * 4 + p % 2 * 2 + st

    barrier = pltpu.get_barrier_semaphore()

    def greet(to):
        pl.semaphore_signal(barrier, inc=1, device_id=to, device_id_type=MESH)

    for d in range(1, 8):
        greet(device(y, (z + d) % 8, xl, c, xh))
        greet(plane((me + d) % 8))
    greet(device(y, z, xl, 1 - c, xh))
    greet(device(home, z, xl, c, 0))
    greet(device(home, z, xl, c, 1))

    sq[...] = jnp.zeros((128, 128), jnp.float32)
    loads = [
        pltpu.make_async_copy(src, dst, isem.at[i])
        for i, (src, dst) in enumerate(
            (
                (re_hbm, sq.at[pl.ds(0, 8)]), (im_hbm, sq.at[pl.ds(64, 8)]), (net_hbm, net_ref),
                (tr_hbm, tr_ref), (qual_hbm, qual_ref), (tw_hbm, tw_ref), (outer_hbm, outer_ref),
            )
        )
    ]
    for load in loads:
        load.start()
    table = pltpu.make_async_copy(inv_hbm, inv, tsem)
    table.start()

    for load in loads[:2]:
        load.wait()
    turned = sq[...].T
    resp = turned[0:16, :]
    for m in range(1, 8):
        resp = resp + pltpu.roll(turned[16 * m : 16 * m + 16, :], 8 * m, 1)
    square = resp * resp
    power = square + swap(square)
    level = 0.1 * (jnp.sum(square) / BINS) + 1e-06
    gbuf[c, z] = jnp.where(low, resp, -resp) / (power + level)
    loads[2].wait()
    row = lax.broadcasted_iota(jnp.int32, (8, 128), 0)
    nbuf[me] = jnp.where(row < 4, net_ref[0], net_ref[1])

    pl.semaphore_wait(barrier, 17)

    def remote(src, dst, ssem, rsem, to):
        return pltpu.make_async_remote_copy(
            src_ref=src, dst_ref=dst, send_sem=ssem, recv_sem=rsem, device_id=to,
            device_id_type=MESH,
        )

    sent = []

    def start(copy):
        copy.start()
        sent.append(copy)

    sibling = device(y, z, xl, 1 - c, xh)
    for d in (4, 3, 5, 2, 6, 1, 7):
        zz = (z + d) % 8
        start(
            remote(gbuf.at[c, z], gbuf.at[c, z], s_r1.at[zz], r_r1.at[z], device(y, zz, xl, c, xh))
        )
    for d in range(1, 8):
        p = (me + d) % 8
        start(remote(nbuf.at[me], nbuf.at[me], s_n.at[p], r_n.at[me], plane(p)))

    for load in loads[3:]:
        load.wait()

    for q in range(10):
        n = min(128, SEG - 128 * q)
        xs[q] = jnp.zeros((8, 128), jnp.float32)
        xs[q, 0:2, 0:n] = tr_ref[:, 128 * q : 128 * q + n]
        xs[q, 2:4, 0:n] = tr_ref[:, SEG + 128 * q : SEG + 128 * q + n]
    for f in range(9):
        parts = []
        for fn, sign in ((math.cos, 1.0), (math.sin, -1.0)):
            total = jnp.zeros((8, 128), jnp.float32)
            for q in range(10):
                w = sign * fn(2 * math.pi * (f * q % 16) / 16)
                if abs(w) > 1e-9:
                    total = total + (xs[q] if w == 1.0 else xs[q] * w)
            parts.append(total)
        for g in {f, (16 - f) % 16}:
            ar, ai = parts if g == f else (parts[0], -parts[1])
            tr, ti = tw_ref[0, g : g + 1, :], tw_ref[1, g : g + 1, :]
            lhs[8 * g : 8 * g + 8, 0:128] = ar * tr - ai * ti
            lhs[8 * g : 8 * g + 8, 128:256] = ar * ti + ai * tr
    xscr[...] = jnp.dot(
        lhs[...], outer_ref[...], precision=HIGHEST, preferred_element_type=jnp.float32
    )
    group = lax.broadcasted_iota(jnp.int32, (8, 128), 1) // 32
    for st in range(2):
        flags = jnp.zeros((8, 128), jnp.float32)
        for g in range(2):
            flag = qual_ref[st, g].astype(jnp.float32)
            xsend[st, 16 * g : 16 * g + 16] = xscr[pl.ds(2 * g + st, 16, stride=8), :] * flag
            flags = jnp.where(group == 2 * xh + g, flag, flags)
        xsend[st, 32:40] = flags

    for st in range(2):
        start(
            remote(xsend.at[st], xrecv.at[xh], s_x.at[st], r_x.at[xh],
                   device(moved(y, st), z, xl, c, y // 2))
        )
    for x in range(2):
        remote(xsend.at[0], xrecv.at[x], s_x.at[0], r_x.at[x], sibling).wait_recv()
    mark = xrecv[0, 32:33, :] + xrecv[1, 32:33, :]
    fa[own] = mark
    fb[c, z] = mark
    for d in range(1, 8):
        zz = (z + d) % 8
        remote(gbuf.at[c, zz], gbuf.at[c, zz], s_r1.at[zz], r_r1.at[zz], sibling).wait_recv()
    start(remote(gbuf.at[c], gbuf.at[c], s_d.at[0], r_d.at[0], sibling))
    for d in range(1, 8):
        zz = (z + d) % 8
        start(remote(fb.at[c, z], fb.at[c, z], s_fb.at[zz], r_fb.at[z], device(y, zz, xl, c, xh)))
    for d in range(1, 8):
        p = (me + d) % 8
        remote(nbuf.at[p], nbuf.at[p], s_n.at[p], r_n.at[p], plane(p)).wait_recv()
    remote(gbuf.at[1 - c], gbuf.at[1 - c], s_d.at[0], r_d.at[0], sibling).wait_recv()

    base = y * 32 + xl * 2

    def choose(p):
        st = which(p // 2, xh)
        want = nbuf[moved(p // 2, st) * 2 + p % 2, pl.ds(4 * st, 1), :]
        acc = jnp.zeros((16, 128), jnp.float32)
        for cc in range(2):
            for zz in range(8):
                acc = jnp.where(want == base + 4 * zz + cc, gbuf[cc, zz], acc)
        return acc

    for d in (4, 5, 3, 2, 6, 1, 7):
        p = (me + d) % 8
        csend[p] = choose(p)
        start(remote(csend.at[p], crecv.at[me], s_r2.at[p], r_r2.at[me], plane(p)))
    factor = choose(me)
    specs = [xrecv[x, 16 * g : 16 * g + 16, :] for x in range(2) for g in range(2)]
    crossed = [swap(spec) for spec in specs]
    for d in range(1, 8):
        p = (me + d) % 8
        remote(csend.at[p], crecv.at[p], s_r2.at[p], r_r2.at[p], plane(p)).wait_recv()
        factor = factor + crecv[p]

    turn = swap(factor)
    f_re = jnp.where(low, factor, turn)
    f_im = jnp.where(low, -turn, factor)
    for s in range(4):
        dec = specs[s] * f_re + crossed[s] * f_im
        square = dec * dec
        energy = square + swap(square)
        mean = jnp.sum(square) / BINS + 1e-06
        white = dec / jnp.sqrt(energy + 0.5 * mean)
        turn = swap(white)
        abuf[own, s] = jnp.concatenate(
            [
                jnp.where(low[0:8], white[0:8], turn[8:16]),
                jnp.where(low[0:8], turn[0:8], white[8:16]),
            ]
        ).astype(jnp.bfloat16)

    for d in (4, 3, 5, 2, 6, 1, 7):
        zz = (z + d) % 8
        start(
            remote(abuf.at[own], bbuf.at[c, z], s_b.at[zz], r_b.at[z], device(y, zz, xl, c, xh))
        )
    for d in (4, 5, 3, 2, 6, 1, 7, 0):
        p = (me + d) % 8
        if d > 0:
            start(
                remote(abuf.at[own], abuf.at[own], s_a.at[p // 2 * 4 + xh * 2 + p % 2], r_a.at[own],
                       plane(p))
            )
        start(
            remote(abuf.at[own], abuf.at[own], s_a.at[p // 2 * 4 + (1 - xh) * 2 + p % 2],
                   r_a.at[own], across(p))
        )
    bbuf[c, z] = abuf[own]

    for d in range(8):
        p = (me + d) % 8
        if d > 0:
            start(
                remote(fa.at[own], fa.at[own], s_fa.at[p // 2 * 4 + xh * 2 + p % 2], r_fa.at[own],
                       plane(p))
            )
        start(
            remote(fa.at[own], fa.at[own], s_fa.at[p // 2 * 4 + (1 - xh) * 2 + p % 2], r_fa.at[own],
                   across(p))
        )
    for d in range(1, 8):
        zz = (z + d) % 8
        remote(fb.at[c, z], fb.at[c, zz], s_fb.at[zz], r_fb.at[zz], sibling).wait_recv()
    start(remote(fb.at[c], fb.at[c], s_d.at[1], r_d.at[1], sibling))

    for d in range(1, 8):
        zz = (z + d) % 8
        remote(abuf.at[own], bbuf.at[c, zz], s_b.at[zz], r_b.at[zz], sibling).wait_recv()
    start(remote(bbuf.at[c], bbuf.at[c], s_d.at[2], r_d.at[2], sibling))
    for d in range(1, 16):
        s = (own + d) % 16
        remote(fa.at[own], fa.at[s], s_fa.at[s], r_fa.at[s], sibling).wait_recv()
    remote(fb.at[1 - c], fb.at[1 - c], s_d.at[1], r_d.at[1], sibling).wait_recv()

    def first_slot(i, st):
        p = (me + i + 3) % 8
        return moved(p // 2, st) * 4 + p // 4 * 2 + p % 2

    for cc in range(2):
        for zz in range(8):
            qa[8 * cc + zz : 8 * cc + zz + 1, :] = fb[cc, zz]
    for i in range(8):
        for st in range(2):
            count = qa[...] * fa[first_slot(i, st)]
            count = count + swap(count)
            count = count + pltpu.roll(count, 32, 1)
            scale[2 * i + st] = 1.0 / jnp.maximum(count, 1.0)

    for d in range(1, 16):
        s = (own + d) % 16
        remote(abuf.at[own], abuf.at[s], s_a.at[s], r_a.at[s], sibling).wait_recv()


    def first(i, _):
        for st in range(2):
            for s in range(4):
                af[2 * i + st, s] = abuf[first_slot(i, st), s].astype(jnp.float32)
        return 0

    lax.fori_loop(0, 8, first, 0)
    remote(bbuf.at[1 - c], bbuf.at[1 - c], s_d.at[2], r_d.at[2], sibling).wait_recv()

    for b in range(16):
        for s in range(4):
            rows[s, 16 * b : 16 * b + 16, :] = bbuf[b // 8, b % 8, s].astype(jnp.float32)
    for s in range(4):
        for r in range(8):
            bf[r, s, 0] = rows[s, pl.ds(r, 16, stride=16), :]
            bf[r, s, 1] = rows[s, pl.ds(r + 8, 16, stride=16), :]

    mine = slot_of(me)
    for lo, hi in PARTS:

        def pairs(r, _, lo=lo, hi=hi):
            other = [(bf[r, s, 0], bf[r, s, 1]) for s in range(4)]
            at = pl.ds(pl.multiple_of(128 * r, 128), 128)
            for a in range(2 * lo, 2 * hi):
                re, im = None, None
                for s in range(4):
                    u, v = af[a, s, pl.ds(r, 1), :], af[a, s, pl.ds(r + 8, 1), :]
                    x, w = other[s]
                    term, turn = u * x + v * w, v * x - u * w
                    re, im = (term, turn) if re is None else (re + term, im + turn)
                to = slice(16 * a, 16 * a + 16)
                mat[0, to, at] = (re * scale[a]).astype(jnp.bfloat16)
                mat[1, to, at] = (im * scale[a]).astype(jnp.bfloat16)
            return 0

        lax.fori_loop(0, 8, pairs, 0)
        if lo == 0:
            table.wait()
        part = slice(32 * lo, 32 * hi)
        for k, (col, at, many) in enumerate(CHUNKS):
            even, odd = [
                jnp.dot(
                    mat[i, part, :], inv[i, :, col : col + 256], preferred_element_type=jnp.float32
                )
                for i in range(2)
            ]
            ahead = (even - odd).astype(jnp.bfloat16)
            back = (even + odd).astype(jnp.bfloat16)
            for i in range(lo, hi):
                to = slice(32 * (i - lo), 32 * (i - lo) + 32)
                if k == 0:
                    sbuf[i, 0:32], sbuf[i, 32:64] = ahead[to, 0:128], ahead[to, 128:256]
                    sbuf[i, 64:96], sbuf[i, 96:128] = back[to, 0:128], back[to, 128:256]
                else:
                    sbuf[i, 128:160], sbuf[i, 160:192] = ahead[to, 0:128], back[to, 0:128]
                    ends = jnp.where(
                        lax.broadcasted_iota(jnp.int32, (32, 128), 1) // 32 % 2 == 0,
                        ahead[to, 128:256].astype(jnp.float32),
                        back[to, 128:256].astype(jnp.float32),
                    )
                    sbuf[i, 192:208] = jnp.where(low, ends[0:16], ends[16:32]).astype(jnp.bfloat16)
                if i != 5:
                    start(
                        remote(sbuf.at[i, pl.ds(at, many)], rbuf.at[mine, pl.ds(at, many)],
                               s_o.at[k, i], r_o.at[k, mine], plane((me + i + 3) % 8))
                    )
    keep = pltpu.make_async_copy(sbuf.at[5], rbuf.at[mine], tsem)
    keep.start()
    keep.wait()
    q, lane = [lax.broadcasted_iota(jnp.int32, (128, 128), i) for i in range(2)]
    ends = q // 64 * 64 + jnp.where(q % 64 < 32, 48 - q % 64, q % 64 - 32)
    ahead, back, ends = [
        jnp.where(lane == to, 1.0, 0.0).astype(jnp.bfloat16) for to in (q, 127 - q, ends)
    ]

    def turned_block(n, at, order):
        for s in range(8):
            for cc in range(2):
                to = s // 4 * 64 + s // 2 % 2 * 4 + s % 2 + cc * 2
                v = rbuf[s, at + 8 * cc : at + 8 * cc + 8, :]
                turn_buf[n, pl.ds(to, 8, stride=8), :] = v.astype(jnp.float32)
        return lax.dot_general(
            order, turn_buf[n].astype(jnp.bfloat16), (((1,), (1,)), ((), ())),
            preferred_element_type=jnp.float32,
        )

    for k, (_, at, many) in enumerate(CHUNKS):
        for d in range(1, 8):
            s = slot_of((me + d) % 8)
            remote(sbuf.at[0, pl.ds(at, many)], rbuf.at[s, pl.ds(at, many)],
                   s_o.at[k, 0], r_o.at[k, s], sibling).wait_recv()
        for a in range(2):
            for n in (0, 1) if k == 0 else (2,):
                to = MAXLAG - 128 * n
                out_ref[to - 127 : to + 1, a, :] = turned_block(
                    4 * n + 2 * a, (64, 96, 160)[n] + 16 * a, back
                )
                to = MAXLAG + 128 * n
                out_ref[to : to + 128, a, :] = turned_block(
                    4 * n + 2 * a + 1, (0, 32, 128)[n] + 16 * a, ahead
                )
        if k == 1:
            v = turned_block(12, 192, ends)
            for a in range(2):
                out_ref[0:17, a, :] = v[64 * a : 64 * a + 17]
                out_ref[784:801, a, :] = v[64 * a + 32 : 64 * a + 49]
    for copy in sent:
        copy.wait_send()


def on_device(traces, response_re, response_im, station_net, quality):
    twiddle, outer, inverse = tables()
    f32, bf16 = jnp.float32, jnp.bfloat16
    dma = pltpu.SemaphoreType.DMA
    lags = pl.pallas_call(
        kernel,
        out_shape=jax.ShapeDtypeStruct((LAGS, 2, 128), f32),
        in_specs=[pl.BlockSpec(memory_space=pltpu.HBM)] * 8,
        out_specs=pl.BlockSpec(memory_space=pltpu.VMEM),
        scratch_shapes=[
            pltpu.SMEM(station_net.shape, jnp.int32),
            pltpu.SMEM(quality.shape, jnp.int32),
            pltpu.VMEM(traces.shape, f32),
            pltpu.VMEM(twiddle.shape, f32),
            pltpu.VMEM(outer.shape, f32),
            pltpu.VMEM(inverse.shape, bf16),
            pltpu.VMEM((10, 8, 128), f32),
            pltpu.VMEM((128, 256), f32),
            pltpu.VMEM((128, 128), f32),
            pltpu.VMEM((128, 128), f32),
            pltpu.VMEM((2, 40, 128), f32),
            pltpu.VMEM((2, 40, 128), f32),
            pltpu.VMEM((2, 8, 16, 128), f32),
            pltpu.VMEM((8, 8, 128), jnp.int32),
            pltpu.VMEM((8, 16, 128), f32),
            pltpu.VMEM((8, 16, 128), f32),
            pltpu.VMEM((16, 1, 128), f32),
            pltpu.VMEM((2, 8, 1, 128), f32),
            pltpu.VMEM((16, 4, 16, 128), bf16),
            pltpu.VMEM((2, 8, 4, 16, 128), bf16),
            pltpu.VMEM((4, 256, 128), f32),
            pltpu.VMEM((16, 4, 16, 128), f32),
            pltpu.VMEM((8, 4, 2, 16, 128), f32),
            pltpu.VMEM((16, 128), f32),
            pltpu.VMEM((16, 16, 128), f32),
            pltpu.VMEM((2, 256, BINS), bf16),
            pltpu.VMEM((8, ROWS, 128), bf16),
            pltpu.VMEM((8, ROWS, 128), bf16),
            pltpu.VMEM((13, 128, 128), f32),
            dma((7,)), dma, dma((2,)), dma((2,)), dma((8,)), dma((8,)), dma((8,)), dma((8,)),
            dma((3,)), dma((3,)), dma((8,)), dma((8,)), dma((16,)), dma((16,)), dma((8,)), dma((8,)),
            dma((16,)), dma((16,)), dma((8,)), dma((8,)), dma((2, 8)), dma((2, 8)),
        ],
        compiler_params=pltpu.CompilerParams(
            collective_id=0, has_side_effects=True, vmem_limit_bytes=40 << 20
        ),
    )(
        *(
            pltpu.with_memory_space_constraint(v, pltpu.HBM)
            for v in (
                station_net, quality, traces, response_re.reshape(8, 128),
                response_im.reshape(8, 128), jnp.asarray(twiddle), jnp.asarray(outer),
                jnp.asarray(inverse),
            )
        )
    )
    return lags.transpose(1, 2, 0)


def solution(mesh):
    return jax.shard_map(
        on_device,
        mesh=mesh,
        in_specs=(P("sta", "win"), P("sta", None), P("sta", None), P("sta"), P("sta", "win")),
        out_specs=P("sta", "win", None),
        check_vma=False,
    )
```

```python
import math

import jax
import jax.numpy as jnp
import ml_dtypes
import numpy as np
from jax import lax
from jax.experimental import pallas as pl
from jax.experimental.pallas import tpu as pltpu
from jax.sharding import PartitionSpec as P

MESH = pl.DeviceIdType.MESH
SEG, BINS, MAXLAG = 1200, 1024, 400
FFT = 2 * BINS
LAGS = 2 * MAXLAG + 1
ROWS = 208
CHUNKS = ((0, 0, 128), (256, 128, 80))
PARTS = ((0, 2), (2, 4), (4, 6), (6, 8))
HIGHEST = lax.Precision.HIGHEST


def tables():
    f1 = np.arange(16)
    lane = np.arange(64)
    f2 = 8 * (lane % 8) + lane // 8
    r = np.arange(128)
    ang = 2 * np.pi * (f1[:, None] * r[None, :] % FFT) / FFT
    twiddle = np.stack([np.cos(ang), -np.sin(ang)]).astype(np.float32)
    ang = 2 * np.pi * (r[:, None] * f2[None, :] % 128) / 128
    c, s = np.cos(ang), np.sin(ang)
    outer = np.concatenate(
        [np.concatenate([c, -s], 1), np.concatenate([s, c], 1)], 0
    ).astype(np.float32)
    f = np.concatenate([f1[:8, None] + 16 * f2, f1[8:, None] + 16 * f2], 1).reshape(BINS)
    k = np.concatenate([np.arange(384), np.tile(384 + np.arange(32), 4)])
    ang = 2 * np.pi * (f[:, None] * k % FFT) / FFT
    w = np.where(f == 0, 1.0, 2.0)[:, None] / math.sqrt(BINS)
    inverse = np.stack([w * np.cos(ang), w * np.sin(ang)]).astype(ml_dtypes.bfloat16)
    return twiddle, outer, inverse


def coords():
    s = lax.axis_index("sta")
    return s // 32, s // 4 % 8, s // 2 % 2, s % 2, lax.axis_index("win")


def device(y, z, xl, c, xh):
    return {"sta": ((y * 8 + z) * 2 + xl) * 2 + c, "win": xh}


def kernel(
    net_hbm, qual_hbm, tr_hbm, re_hbm, im_hbm, tw_hbm, outer_hbm, inv_hbm, out_ref,
    net_ref, qual_ref, tr_ref, tw_ref, outer_ref, inv,
    xs, lhs, xscr, sq, xsend, xrecv, gbuf, nbuf, csend, crecv, fa, fb, abuf, bbuf, rows, af, bf, qa, scale, mat, sbuf, rbuf, turn_buf,
    isem, tsem, s_x, r_x, s_r1, r_r1, s_n, r_n, s_d, r_d, s_r2, r_r2, s_fa, r_fa, s_fb, r_fb, s_a, r_a, s_b, r_b,
    s_o, r_o,
):
    y, z, xl, c, xh = coords()
    me = y * 2 + xl
    own = y * 4 + xh * 2 + xl
    lane = lax.broadcasted_iota(jnp.int32, (16, 128), 1)
    low = lane < 64

    def swap(v):
        return pltpu.roll(v, 64, 1)

    def plane(p):
        return device(p // 2, z, p % 2, c, xh)

    def across(p):
        return device(p // 2, z, p % 2, c, 1 - xh)

    def moved(yy, st):
        return yy + (1 - 2 * (yy % 2)) * (1 - st) + (3 - 2 * yy) * st

    def which(yy, hh):
        return (yy // 2 + hh) % 2

    st_own = which(y, xh)
    home = moved(y, st_own)

    def slot_of(p):
        st = which(p // 2, xh)
        return (moved(p // 2, st) % 2) * 4 + p % 2 * 2 + st

    barrier = pltpu.get_barrier_semaphore()

    def greet(to):
        pl.semaphore_signal(barrier, inc=1, device_id=to, device_id_type=MESH)

    for d in (4, 3, 5, 2, 6, 1, 7):
        greet(device(y, (z + d) % 8, xl, c, xh))
    greet(device(home, z, xl, c, 0))
    greet(device(home, z, xl, c, 1))
    for d in (4, 5, 3, 2, 6, 1, 7):
        greet(plane((me + d) % 8))
    greet(device(y, z, xl, 1 - c, xh))

    sq[...] = jnp.zeros((128, 128), jnp.float32)
    loads = [
        pltpu.make_async_copy(src, dst, isem.at[i])
        for i, (src, dst) in enumerate(
            (
                (re_hbm, sq.at[pl.ds(0, 8)]), (im_hbm, sq.at[pl.ds(64, 8)]), (net_hbm, net_ref),
                (tr_hbm, tr_ref), (qual_hbm, qual_ref), (tw_hbm, tw_ref), (outer_hbm, outer_ref),
            )
        )
    ]
    for load in loads:
        load.start()
    table = pltpu.make_async_copy(inv_hbm, inv, tsem)
    table.start()

    for load in loads[:2]:
        load.wait()
    turned = sq[...].T
    resp = turned[0:16, :]
    for m in range(1, 8):
        resp = resp + pltpu.roll(turned[16 * m : 16 * m + 16, :], 8 * m, 1)
    square = resp * resp
    power = square + swap(square)
    level = 0.1 * (jnp.sum(square) / BINS) + 1e-06
    gbuf[c, z] = jnp.where(low, resp, -resp) / (power + level)
    loads[2].wait()
    row = lax.broadcasted_iota(jnp.int32, (8, 128), 0)
    nbuf[me] = jnp.where(row < 4, net_ref[0], net_ref[1])

    pl.semaphore_wait(barrier, 17)

    def remote(src, dst, ssem, rsem, to):
        return pltpu.make_async_remote_copy(
            src_ref=src, dst_ref=dst, send_sem=ssem, recv_sem=rsem, device_id=to,
            device_id_type=MESH,
        )

    sent = []

    def start(copy):
        copy.start()
        sent.append(copy)

    sibling = device(y, z, xl, 1 - c, xh)
    for d in (4, 3, 5, 2, 6, 1, 7):
        zz = (z + d) % 8
        start(
            remote(gbuf.at[c, z], gbuf.at[c, z], s_r1.at[zz], r_r1.at[z], device(y, zz, xl, c, xh))
        )
    for d in range(1, 8):
        p = (me + d) % 8
        start(remote(nbuf.at[me], nbuf.at[me], s_n.at[p], r_n.at[me], plane(p)))

    for load in loads[3:]:
        load.wait()

    for q in range(10):
        n = min(128, SEG - 128 * q)
        xs[q] = jnp.zeros((8, 128), jnp.float32)
        xs[q, 0:2, 0:n] = tr_ref[:, 128 * q : 128 * q + n]
        xs[q, 2:4, 0:n] = tr_ref[:, SEG + 128 * q : SEG + 128 * q + n]
    for f in range(9):
        parts = []
        for fn, sign in ((math.cos, 1.0), (math.sin, -1.0)):
            total = jnp.zeros((8, 128), jnp.float32)
            for q in range(10):
                w = sign * fn(2 * math.pi * (f * q % 16) / 16)
                if abs(w) > 1e-9:
                    total = total + (xs[q] if w == 1.0 else xs[q] * w)
            parts.append(total)
        for g in {f, (16 - f) % 16}:
            ar, ai = parts if g == f else (parts[0], -parts[1])
            tr, ti = tw_ref[0, g : g + 1, :], tw_ref[1, g : g + 1, :]
            lhs[8 * g : 8 * g + 8, 0:128] = ar * tr - ai * ti
            lhs[8 * g : 8 * g + 8, 128:256] = ar * ti + ai * tr
    xscr[0:128, :] = jnp.dot(
        lhs[...], outer_ref[...], precision=HIGHEST, preferred_element_type=jnp.float32
    )
    group = lax.broadcasted_iota(jnp.int32, (8, 128), 1) // 32
    for st in range(2):
        flags = jnp.zeros((8, 128), jnp.float32)
        for g in range(2):
            flag = qual_ref[st, g].astype(jnp.float32)
            xsend[st, 16 * g : 16 * g + 16] = xscr[pl.ds(2 * g + st, 16, stride=8), :] * flag
            flags = jnp.where(group == 2 * xh + g, flag, flags)
        xsend[st, 32:40] = flags

    for st in range(2):
        start(
            remote(xsend.at[st], xrecv.at[xh], s_x.at[st], r_x.at[xh],
                   device(moved(y, st), z, xl, c, y // 2))
        )
    for x in range(2):
        remote(xsend.at[0], xrecv.at[x], s_x.at[0], r_x.at[x], sibling).wait_recv()
    mark = xrecv[0, 32:33, :] + xrecv[1, 32:33, :]
    fa[own] = mark
    fb[c, z] = mark
    for d in range(1, 8):
        zz = (z + d) % 8
        remote(gbuf.at[c, zz], gbuf.at[c, zz], s_r1.at[zz], r_r1.at[zz], sibling).wait_recv()
    start(remote(gbuf.at[c], gbuf.at[c], s_d.at[0], r_d.at[0], sibling))
    for d in range(1, 8):
        zz = (z + d) % 8
        start(remote(fb.at[c, z], fb.at[c, z], s_fb.at[zz], r_fb.at[z], device(y, zz, xl, c, xh)))
    for d in range(1, 8):
        p = (me + d) % 8
        remote(nbuf.at[p], nbuf.at[p], s_n.at[p], r_n.at[p], plane(p)).wait_recv()
    remote(gbuf.at[1 - c], gbuf.at[1 - c], s_d.at[0], r_d.at[0], sibling).wait_recv()

    base = y * 32 + xl * 2

    def choose(p):
        st = which(p // 2, xh)
        want = nbuf[moved(p // 2, st) * 2 + p % 2, pl.ds(4 * st, 1), :]
        acc = jnp.zeros((16, 128), jnp.float32)
        for cc in range(2):
            for zz in range(8):
                acc = jnp.where(want == base + 4 * zz + cc, gbuf[cc, zz], acc)
        return acc

    for d in (4, 5, 3, 2, 6, 1, 7):
        p = (me + d) % 8
        csend[p] = choose(p)
        start(remote(csend.at[p], crecv.at[me], s_r2.at[p], r_r2.at[me], plane(p)))
    factor = choose(me)
    specs = [xrecv[x, 16 * g : 16 * g + 16, :] for x in range(2) for g in range(2)]
    crossed = [swap(spec) for spec in specs]
    for d in range(1, 8):
        p = (me + d) % 8
        remote(csend.at[p], crecv.at[p], s_r2.at[p], r_r2.at[p], plane(p)).wait_recv()
        factor = factor + crecv[p]

    turn = swap(factor)
    f_re = jnp.where(low, factor, turn)
    f_im = jnp.where(low, -turn, factor)
    for s in range(4):
        dec = specs[s] * f_re + crossed[s] * f_im
        square = dec * dec
        energy = square + swap(square)
        mean = jnp.sum(square) / BINS + 1e-06
        white = dec / jnp.sqrt(energy + 0.5 * mean)
        turn = swap(white)
        abuf[own, s] = jnp.concatenate(
            [
                jnp.where(low[0:8], white[0:8], turn[8:16]),
                jnp.where(low[0:8], turn[0:8], white[8:16]),
            ]
        ).astype(jnp.bfloat16)

    for d in (4, 3, 5, 2, 6, 1, 7):
        zz = (z + d) % 8
        start(
            remote(abuf.at[own], bbuf.at[c, z], s_b.at[zz], r_b.at[z], device(y, zz, xl, c, xh))
        )
    for d in (4, 5, 3, 2, 6, 1, 7, 0):
        p = (me + d) % 8
        if d > 0:
            start(
                remote(abuf.at[own], abuf.at[own], s_a.at[p // 2 * 4 + xh * 2 + p % 2], r_a.at[own],
                       plane(p))
            )
        start(
            remote(abuf.at[own], abuf.at[own], s_a.at[p // 2 * 4 + (1 - xh) * 2 + p % 2],
                   r_a.at[own], across(p))
        )
    bbuf[c, z] = abuf[own]

    for d in range(8):
        p = (me + d) % 8
        if d > 0:
            start(
                remote(fa.at[own], fa.at[own], s_fa.at[p // 2 * 4 + xh * 2 + p % 2], r_fa.at[own],
                       plane(p))
            )
        start(
            remote(fa.at[own], fa.at[own], s_fa.at[p // 2 * 4 + (1 - xh) * 2 + p % 2], r_fa.at[own],
                   across(p))
        )
    for d in range(1, 8):
        zz = (z + d) % 8
        remote(fb.at[c, z], fb.at[c, zz], s_fb.at[zz], r_fb.at[zz], sibling).wait_recv()
    start(remote(fb.at[c], fb.at[c], s_d.at[1], r_d.at[1], sibling))

    for d in range(1, 8):
        zz = (z + d) % 8
        remote(abuf.at[own], bbuf.at[c, zz], s_b.at[zz], r_b.at[zz], sibling).wait_recv()
    start(remote(bbuf.at[c], bbuf.at[c], s_d.at[2], r_d.at[2], sibling))
    for d in range(1, 16):
        s = (own + d) % 16
        remote(fa.at[own], fa.at[s], s_fa.at[s], r_fa.at[s], sibling).wait_recv()
    remote(fb.at[1 - c], fb.at[1 - c], s_d.at[1], r_d.at[1], sibling).wait_recv()

    def first_slot(i, st):
        p = (me + i + 3) % 8
        return moved(p // 2, st) * 4 + p // 4 * 2 + p % 2

    for cc in range(2):
        for zz in range(8):
            qa[8 * cc + zz : 8 * cc + zz + 1, :] = fb[cc, zz]
    for i in range(8):
        for st in range(2):
            count = qa[...] * fa[first_slot(i, st)]
            count = count + swap(count)
            count = count + pltpu.roll(count, 32, 1)
            scale[2 * i + st] = 1.0 / jnp.maximum(count, 1.0)

    for d in range(1, 16):
        s = (own + d) % 16
        remote(abuf.at[own], abuf.at[s], s_a.at[s], r_a.at[s], sibling).wait_recv()


    def first(i, _):
        for st in range(2):
            for s in range(4):
                af[2 * i + st, s] = abuf[first_slot(i, st), s].astype(jnp.float32)
        return 0

    lax.fori_loop(0, 8, first, 0)
    def second(cc):
        for zz in range(8):
            for s in range(4):
                at = pl.multiple_of(128 * cc + 16 * zz, 16)
                rows[s, pl.ds(at, 16), :] = bbuf[cc, zz, s].astype(jnp.float32)
        for s in range(4):
            for r in range(8):
                for k in range(2):
                    bf[r, s, k, pl.ds(pl.multiple_of(8 * cc, 8), 8), :] = rows[
                        s, pl.ds(128 * cc + r + 8 * k, 8, stride=16), :
                    ]

    second(c)
    remote(bbuf.at[1 - c], bbuf.at[1 - c], s_d.at[2], r_d.at[2], sibling).wait_recv()
    second(1 - c)

    mine = slot_of(me)
    for lo, hi in PARTS:

        def pairs(r, _, lo=lo, hi=hi):
            other = [(bf[r, s, 0], bf[r, s, 1]) for s in range(4)]
            at = pl.ds(pl.multiple_of(128 * r, 128), 128)
            for a in range(2 * lo, 2 * hi):
                re, im = None, None
                for s in range(4):
                    u, v = af[a, s, pl.ds(r, 1), :], af[a, s, pl.ds(r + 8, 1), :]
                    x, w = other[s]
                    term, turn = u * x + v * w, v * x - u * w
                    re, im = (term, turn) if re is None else (re + term, im + turn)
                to = slice(16 * a, 16 * a + 16)
                mat[0, to, at] = (re * scale[a]).astype(jnp.bfloat16)
                mat[1, to, at] = (im * scale[a]).astype(jnp.bfloat16)
            return 0

        lax.fori_loop(0, 8, pairs, 0)
        if lo == 0:
            table.wait()
        part = slice(32 * lo, 32 * hi)
        for k, (col, at, many) in enumerate(CHUNKS):
            even, odd = [
                jnp.dot(
                    mat[i, part, :], inv[i, :, col : col + 256], preferred_element_type=jnp.float32
                )
                for i in range(2)
            ]
            ahead = (even - odd).astype(jnp.bfloat16)
            back = (even + odd).astype(jnp.bfloat16)
            for i in range(lo, hi):
                to = slice(32 * (i - lo), 32 * (i - lo) + 32)
                if k == 0:
                    sbuf[i, 0:32], sbuf[i, 32:64] = ahead[to, 0:128], ahead[to, 128:256]
                    sbuf[i, 64:96], sbuf[i, 96:128] = back[to, 0:128], back[to, 128:256]
                else:
                    sbuf[i, 128:160], sbuf[i, 160:192] = ahead[to, 0:128], back[to, 0:128]
                    ends = jnp.where(
                        lax.broadcasted_iota(jnp.int32, (32, 128), 1) // 32 % 2 == 0,
                        ahead[to, 128:256].astype(jnp.float32),
                        back[to, 128:256].astype(jnp.float32),
                    )
                    sbuf[i, 192:208] = jnp.where(low, ends[0:16], ends[16:32]).astype(jnp.bfloat16)
                if i != 5:
                    start(
                        remote(sbuf.at[i, pl.ds(at, many)], rbuf.at[mine, pl.ds(at, many)],
                               s_o.at[k, i], r_o.at[k, mine], plane((me + i + 3) % 8))
                    )
    keep = pltpu.make_async_copy(sbuf.at[5], rbuf.at[mine], tsem)
    keep.start()
    keep.wait()
    q, lane = [lax.broadcasted_iota(jnp.int32, (128, 128), i) for i in range(2)]
    ends = q // 64 * 64 + jnp.where(q % 64 < 32, 48 - q % 64, q % 64 - 32)
    ahead, back, ends = [
        jnp.where(lane == to, 1.0, 0.0).astype(jnp.bfloat16) for to in (q, 127 - q, ends)
    ]

    def turned_block(n, at, order):
        for s in range(8):
            for cc in range(2):
                to = s // 4 * 64 + s // 2 % 2 * 4 + s % 2 + cc * 2
                v = rbuf[s, at + 8 * cc : at + 8 * cc + 8, :]
                turn_buf[n, pl.ds(to, 8, stride=8), :] = v.astype(jnp.float32)
        return lax.dot_general(
            order, turn_buf[n, 0:128, :].astype(jnp.bfloat16), (((1,), (1,)), ((), ())),
            preferred_element_type=jnp.float32,
        )

    for k, (_, at, many) in enumerate(CHUNKS):
        for d in range(1, 8):
            s = slot_of((me + d) % 8)
            remote(sbuf.at[0, pl.ds(at, many)], rbuf.at[s, pl.ds(at, many)],
                   s_o.at[k, 0], r_o.at[k, s], sibling).wait_recv()
        for a in range(2):
            for n in (0, 1) if k == 0 else (2,):
                to = MAXLAG - 128 * n
                out_ref[to - 127 : to + 1, a, :] = turned_block(
                    4 * n + 2 * a, (64, 96, 160)[n] + 16 * a, back
                )
                to = MAXLAG + 128 * n
                out_ref[to : to + 128, a, :] = turned_block(
                    4 * n + 2 * a + 1, (0, 32, 128)[n] + 16 * a, ahead
                )
        if k == 1:
            v = turned_block(12, 192, ends)
            for a in range(2):
                out_ref[0:17, a, :] = v[64 * a : 64 * a + 17]
                out_ref[784:801, a, :] = v[64 * a + 32 : 64 * a + 49]
    for copy in sent:
        copy.wait_send()


def on_device(traces, response_re, response_im, station_net, quality):
    twiddle, outer, inverse = tables()
    f32, bf16 = jnp.float32, jnp.bfloat16
    dma = pltpu.SemaphoreType.DMA
    lags = pl.pallas_call(
        kernel,
        out_shape=jax.ShapeDtypeStruct((LAGS, 2, 128), f32),
        in_specs=[pl.BlockSpec(memory_space=pltpu.HBM)] * 8,
        out_specs=pl.BlockSpec(memory_space=pltpu.VMEM),
        scratch_shapes=[
            pltpu.SMEM(station_net.shape, jnp.int32),
            pltpu.SMEM(quality.shape, jnp.int32),
            pltpu.VMEM(traces.shape, f32),
            pltpu.VMEM(twiddle.shape, f32),
            pltpu.VMEM(outer.shape, f32),
            pltpu.VMEM(inverse.shape, bf16),
            pltpu.VMEM((10, 8, 128), f32),
            pltpu.VMEM((128, 256), f32),
            pltpu.VMEM((136, 128), f32),
            pltpu.VMEM((128, 128), f32),
            pltpu.VMEM((2, 40, 128), f32),
            pltpu.VMEM((2, 40, 128), f32),
            pltpu.VMEM((2, 8, 16, 128), f32),
            pltpu.VMEM((8, 8, 128), jnp.int32),
            pltpu.VMEM((8, 16, 128), f32),
            pltpu.VMEM((8, 16, 128), f32),
            pltpu.VMEM((16, 1, 128), f32),
            pltpu.VMEM((2, 8, 1, 128), f32),
            pltpu.VMEM((16, 4, 16, 128), bf16),
            pltpu.VMEM((2, 8, 4, 16, 128), bf16),
            pltpu.VMEM((4, 272, 128), f32),
            pltpu.VMEM((16, 4, 16, 128), f32),
            pltpu.VMEM((8, 4, 2, 16, 128), f32),
            pltpu.VMEM((16, 128), f32),
            pltpu.VMEM((16, 16, 128), f32),
            pltpu.VMEM((2, 256, BINS), bf16),
            pltpu.VMEM((8, ROWS, 128), bf16),
            pltpu.VMEM((8, ROWS, 128), bf16),
            pltpu.VMEM((13, 136, 128), f32),
            dma((7,)), dma, dma((2,)), dma((2,)), dma((8,)), dma((8,)), dma((8,)), dma((8,)),
            dma((3,)), dma((3,)), dma((8,)), dma((8,)), dma((16,)), dma((16,)), dma((8,)), dma((8,)),
            dma((16,)), dma((16,)), dma((8,)), dma((8,)), dma((2, 8)), dma((2, 8)),
        ],
        compiler_params=pltpu.CompilerParams(
            collective_id=0, has_side_effects=True, vmem_limit_bytes=40 << 20
        ),
    )(
        *(
            pltpu.with_memory_space_constraint(v, pltpu.HBM)
            for v in (
                station_net, quality, traces, response_re.reshape(8, 128),
                response_im.reshape(8, 128), jnp.asarray(twiddle), jnp.asarray(outer),
                jnp.asarray(inverse),
            )
        )
    )
    return lags.transpose(1, 2, 0)


def solution(mesh):
    return jax.shard_map(
        on_device,
        mesh=mesh,
        in_specs=(P("sta", "win"), P("sta", None), P("sta", None), P("sta"), P("sta", "win")),
        out_specs=P("sta", "win", None),
        check_vma=False,
    )
```

```python
import math

import jax
import jax.numpy as jnp
import ml_dtypes
import numpy as np
from jax import lax
from jax.experimental import pallas as pl
from jax.experimental.pallas import tpu as pltpu
from jax.sharding import PartitionSpec as P

MESH = pl.DeviceIdType.MESH
SEG, BINS, MAXLAG = 1200, 1024, 400
FFT = 2 * BINS
LAGS = 2 * MAXLAG + 1
ROWS = 208
CHUNKS = ((0, 0, 128), (256, 128, 80))
PARTS = ((0, 1), (1, 3), (3, 5), (5, 8))
HIGHEST = lax.Precision.HIGHEST


def tables():
    f1 = np.arange(16)
    lane = np.arange(64)
    f2 = 8 * (lane % 8) + lane // 8
    r = np.arange(128)
    ang = 2 * np.pi * (f1[:, None] * r[None, :] % FFT) / FFT
    twiddle = np.stack([np.cos(ang), -np.sin(ang)]).astype(np.float32)
    ang = 2 * np.pi * (r[:, None] * f2[None, :] % 128) / 128
    c, s = np.cos(ang), np.sin(ang)
    outer = np.concatenate(
        [np.concatenate([c, -s], 1), np.concatenate([s, c], 1)], 0
    ).astype(np.float32)
    f = np.concatenate([f1[:8, None] + 16 * f2, f1[8:, None] + 16 * f2], 1).reshape(BINS)
    k = np.concatenate([np.arange(384), np.tile(384 + np.arange(32), 4)])
    ang = 2 * np.pi * (f[:, None] * k % FFT) / FFT
    w = np.where(f == 0, 1.0, 2.0)[:, None] / math.sqrt(BINS)
    inverse = np.stack([w * np.cos(ang), w * np.sin(ang)]).astype(ml_dtypes.bfloat16)
    return twiddle, outer, inverse


def coords():
    s = lax.axis_index("sta")
    return s // 32, s // 4 % 8, s // 2 % 2, s % 2, lax.axis_index("win")


def device(y, z, xl, c, xh):
    return {"sta": ((y * 8 + z) * 2 + xl) * 2 + c, "win": xh}


def kernel(
    net_hbm, qual_hbm, tr_hbm, re_hbm, im_hbm, tw_hbm, outer_hbm, inv_hbm, out_ref,
    net_ref, qual_ref, tr_ref, tw_ref, outer_ref, inv,
    xs, lhs, xscr, sq, xsend, xrecv, gbuf, nbuf, csend, crecv, fa, fb, abuf, bbuf, rows, af, bf, qa, scale, mat, sbuf, rbuf, turn_buf,
    isem, tsem, s_x, r_x, s_r1, r_r1, s_n, r_n, s_d, r_d, s_r2, r_r2, s_fa, r_fa, s_fb, r_fb, s_a, r_a, s_b, r_b,
    s_o, r_o,
):
    y, z, xl, c, xh = coords()
    me = y * 2 + xl
    own = y * 4 + xh * 2 + xl
    lane = lax.broadcasted_iota(jnp.int32, (16, 128), 1)
    low = lane < 64

    def swap(v):
        return pltpu.roll(v, 64, 1)

    def plane(p):
        return device(p // 2, z, p % 2, c, xh)

    def across(p):
        return device(p // 2, z, p % 2, c, 1 - xh)

    def moved(yy, st):
        return yy + (1 - 2 * (yy % 2)) * (1 - st) + (3 - 2 * yy) * st

    def which(yy, hh):
        return (yy // 2 + hh) % 2

    st_own = which(y, xh)
    home = moved(y, st_own)

    def slot_of(p):
        st = which(p // 2, xh)
        return (moved(p // 2, st) % 2) * 4 + p % 2 * 2 + st

    barrier = pltpu.get_barrier_semaphore()

    def greet(to):
        pl.semaphore_signal(barrier, inc=1, device_id=to, device_id_type=MESH)

    for d in (4, 3, 5, 2, 6, 1, 7):
        greet(device(y, (z + d) % 8, xl, c, xh))
    greet(device(home, z, xl, c, 0))
    greet(device(home, z, xl, c, 1))
    for d in (4, 5, 3, 2, 6, 1, 7):
        greet(plane((me + d) % 8))
    greet(device(y, z, xl, 1 - c, xh))

    sq[...] = jnp.zeros((128, 128), jnp.float32)
    loads = [
        pltpu.make_async_copy(src, dst, isem.at[i])
        for i, (src, dst) in enumerate(
            (
                (re_hbm, sq.at[pl.ds(0, 8)]), (im_hbm, sq.at[pl.ds(64, 8)]), (net_hbm, net_ref),
                (tr_hbm, tr_ref), (qual_hbm, qual_ref), (tw_hbm, tw_ref), (outer_hbm, outer_ref),
            )
        )
    ]
    for load in loads:
        load.start()
    table = pltpu.make_async_copy(inv_hbm, inv, tsem)
    table.start()

    for load in loads[:2]:
        load.wait()
    turned = sq[...].T
    resp = turned[0:16, :]
    for m in range(1, 8):
        resp = resp + pltpu.roll(turned[16 * m : 16 * m + 16, :], 8 * m, 1)
    square = resp * resp
    power = square + swap(square)
    level = 0.1 * (jnp.sum(square) / BINS) + 1e-06
    gbuf[c, z] = jnp.where(low, resp, -resp) / (power + level)
    loads[2].wait()
    row = lax.broadcasted_iota(jnp.int32, (8, 128), 0)
    nbuf[me] = jnp.where(row < 4, net_ref[0], net_ref[1])

    pl.semaphore_wait(barrier, 17)

    def remote(src, dst, ssem, rsem, to):
        return pltpu.make_async_remote_copy(
            src_ref=src, dst_ref=dst, send_sem=ssem, recv_sem=rsem, device_id=to,
            device_id_type=MESH,
        )

    sent = []

    def start(copy):
        copy.start()
        sent.append(copy)

    sibling = device(y, z, xl, 1 - c, xh)
    for d in (4, 3, 5, 2, 6, 1, 7):
        zz = (z + d) % 8
        start(
            remote(gbuf.at[c, z], gbuf.at[c, z], s_r1.at[zz], r_r1.at[z], device(y, zz, xl, c, xh))
        )
    for d in range(1, 8):
        p = (me + d) % 8
        start(remote(nbuf.at[me], nbuf.at[me], s_n.at[p], r_n.at[me], plane(p)))

    for load in loads[3:]:
        load.wait()

    for q in range(10):
        n = min(128, SEG - 128 * q)
        xs[q] = jnp.zeros((8, 128), jnp.float32)
        xs[q, 0:2, 0:n] = tr_ref[:, 128 * q : 128 * q + n]
        xs[q, 2:4, 0:n] = tr_ref[:, SEG + 128 * q : SEG + 128 * q + n]
    for f in range(9):
        parts = []
        for fn, sign in ((math.cos, 1.0), (math.sin, -1.0)):
            total = jnp.zeros((8, 128), jnp.float32)
            for q in range(10):
                w = sign * fn(2 * math.pi * (f * q % 16) / 16)
                if abs(w) > 1e-9:
                    total = total + (xs[q] if w == 1.0 else xs[q] * w)
            parts.append(total)
        for g in {f, (16 - f) % 16}:
            ar, ai = parts if g == f else (parts[0], -parts[1])
            tr, ti = tw_ref[0, g : g + 1, :], tw_ref[1, g : g + 1, :]
            lhs[8 * g : 8 * g + 8, 0:128] = ar * tr - ai * ti
            lhs[8 * g : 8 * g + 8, 128:256] = ar * ti + ai * tr
    xscr[0:128, :] = jnp.dot(
        lhs[...], outer_ref[...], precision=HIGHEST, preferred_element_type=jnp.float32
    )
    group = lax.broadcasted_iota(jnp.int32, (8, 128), 1) // 32
    for st in range(2):
        flags = jnp.zeros((8, 128), jnp.float32)
        for g in range(2):
            flag = qual_ref[st, g].astype(jnp.float32)
            xsend[st, 16 * g : 16 * g + 16] = xscr[pl.ds(2 * g + st, 16, stride=8), :] * flag
            flags = jnp.where(group == 2 * xh + g, flag, flags)
        xsend[st, 32:40] = flags

    for st in range(2):
        start(
            remote(xsend.at[st], xrecv.at[xh], s_x.at[st], r_x.at[xh],
                   device(moved(y, st), z, xl, c, y // 2))
        )
    for x in range(2):
        remote(xsend.at[0], xrecv.at[x], s_x.at[0], r_x.at[x], sibling).wait_recv()
    mark = xrecv[0, 32:33, :] + xrecv[1, 32:33, :]
    fa[own] = mark
    fb[c, z] = mark
    for d in range(1, 8):
        zz = (z + d) % 8
        remote(gbuf.at[c, zz], gbuf.at[c, zz], s_r1.at[zz], r_r1.at[zz], sibling).wait_recv()
    start(remote(gbuf.at[c], gbuf.at[c], s_d.at[0], r_d.at[0], sibling))
    for d in range(1, 8):
        zz = (z + d) % 8
        start(remote(fb.at[c, z], fb.at[c, z], s_fb.at[zz], r_fb.at[z], device(y, zz, xl, c, xh)))
    for d in range(1, 8):
        p = (me + d) % 8
        remote(nbuf.at[p], nbuf.at[p], s_n.at[p], r_n.at[p], plane(p)).wait_recv()
    remote(gbuf.at[1 - c], gbuf.at[1 - c], s_d.at[0], r_d.at[0], sibling).wait_recv()

    base = y * 32 + xl * 2

    def choose(p):
        st = which(p // 2, xh)
        want = nbuf[moved(p // 2, st) * 2 + p % 2, pl.ds(4 * st, 1), :]
        acc = jnp.zeros((16, 128), jnp.float32)
        for cc in range(2):
            for zz in range(8):
                acc = jnp.where(want == base + 4 * zz + cc, gbuf[cc, zz], acc)
        return acc

    for d in (4, 5, 3, 2, 6, 1, 7):
        p = (me + d) % 8
        csend[p] = choose(p)
        start(remote(csend.at[p], crecv.at[me], s_r2.at[p], r_r2.at[me], plane(p)))
    factor = choose(me)
    specs = [xrecv[x, 16 * g : 16 * g + 16, :] for x in range(2) for g in range(2)]
    crossed = [swap(spec) for spec in specs]
    for d in range(1, 8):
        p = (me + d) % 8
        remote(csend.at[p], crecv.at[p], s_r2.at[p], r_r2.at[p], plane(p)).wait_recv()
        factor = factor + crecv[p]

    turn = swap(factor)
    f_re = jnp.where(low, factor, turn)
    f_im = jnp.where(low, -turn, factor)
    for s in range(4):
        dec = specs[s] * f_re + crossed[s] * f_im
        square = dec * dec
        energy = square + swap(square)
        mean = jnp.sum(square) / BINS + 1e-06
        white = dec / jnp.sqrt(energy + 0.5 * mean)
        turn = swap(white)
        abuf[own, s] = jnp.concatenate(
            [
                jnp.where(low[0:8], white[0:8], turn[8:16]),
                jnp.where(low[0:8], turn[0:8], white[8:16]),
            ]
        ).astype(jnp.bfloat16)

    for d in (4, 3, 5, 2, 6, 1, 7):
        zz = (z + d) % 8
        start(
            remote(abuf.at[own], bbuf.at[c, z], s_b.at[zz], r_b.at[z], device(y, zz, xl, c, xh))
        )
    for d in (4, 5, 3, 2, 6, 1, 7, 0):
        p = (me + d) % 8
        if d > 0:
            start(
                remote(abuf.at[own], abuf.at[own], s_a.at[p // 2 * 4 + xh * 2 + p % 2], r_a.at[own],
                       plane(p))
            )
        start(
            remote(abuf.at[own], abuf.at[own], s_a.at[p // 2 * 4 + (1 - xh) * 2 + p % 2],
                   r_a.at[own], across(p))
        )
    bbuf[c, z] = abuf[own]

    for d in range(8):
        p = (me + d) % 8
        if d > 0:
            start(
                remote(fa.at[own], fa.at[own], s_fa.at[p // 2 * 4 + xh * 2 + p % 2], r_fa.at[own],
                       plane(p))
            )
        start(
            remote(fa.at[own], fa.at[own], s_fa.at[p // 2 * 4 + (1 - xh) * 2 + p % 2], r_fa.at[own],
                   across(p))
        )
    for d in range(1, 8):
        zz = (z + d) % 8
        remote(fb.at[c, z], fb.at[c, zz], s_fb.at[zz], r_fb.at[zz], sibling).wait_recv()
    start(remote(fb.at[c], fb.at[c], s_d.at[1], r_d.at[1], sibling))

    for d in range(1, 8):
        zz = (z + d) % 8
        remote(abuf.at[own], bbuf.at[c, zz], s_b.at[zz], r_b.at[zz], sibling).wait_recv()
    start(remote(bbuf.at[c], bbuf.at[c], s_d.at[2], r_d.at[2], sibling))
    for d in range(1, 16):
        s = (own + d) % 16
        remote(fa.at[own], fa.at[s], s_fa.at[s], r_fa.at[s], sibling).wait_recv()
    remote(fb.at[1 - c], fb.at[1 - c], s_d.at[1], r_d.at[1], sibling).wait_recv()

    def first_slot(i, st):
        p = (me + i + 3) % 8
        return moved(p // 2, st) * 4 + p // 4 * 2 + p % 2

    for cc in range(2):
        for zz in range(8):
            qa[8 * cc + zz : 8 * cc + zz + 1, :] = fb[cc, zz]
    for i in range(8):
        for st in range(2):
            count = qa[...] * fa[first_slot(i, st)]
            count = count + swap(count)
            count = count + pltpu.roll(count, 32, 1)
            scale[2 * i + st] = 1.0 / jnp.maximum(count, 1.0)

    for d in range(1, 16):
        s = (own + d) % 16
        remote(abuf.at[own], abuf.at[s], s_a.at[s], r_a.at[s], sibling).wait_recv()


    def first(i, _):
        for st in range(2):
            for s in range(4):
                af[2 * i + st, s] = abuf[first_slot(i, st), s].astype(jnp.float32)
        return 0

    lax.fori_loop(0, 8, first, 0)
    def second(cc):
        for zz in range(8):
            for s in range(4):
                at = pl.multiple_of(128 * cc + 16 * zz, 16)
                rows[s, pl.ds(at, 16), :] = bbuf[cc, zz, s].astype(jnp.float32)
        for s in range(4):
            for r in range(8):
                for k in range(2):
                    bf[r, s, k, pl.ds(pl.multiple_of(8 * cc, 8), 8), :] = rows[
                        s, pl.ds(128 * cc + r + 8 * k, 8, stride=16), :
                    ]

    second(c)
    remote(bbuf.at[1 - c], bbuf.at[1 - c], s_d.at[2], r_d.at[2], sibling).wait_recv()
    second(1 - c)

    mine = slot_of(me)
    for lo, hi in PARTS:

        def pairs(r, _, lo=lo, hi=hi):
            other = [(bf[r, s, 0], bf[r, s, 1]) for s in range(4)]
            at = pl.ds(pl.multiple_of(128 * r, 128), 128)
            for a in range(2 * lo, 2 * hi):
                re, im = None, None
                for s in range(4):
                    u, v = af[a, s, pl.ds(r, 1), :], af[a, s, pl.ds(r + 8, 1), :]
                    x, w = other[s]
                    term, turn = u * x + v * w, v * x - u * w
                    re, im = (term, turn) if re is None else (re + term, im + turn)
                to = slice(16 * a, 16 * a + 16)
                mat[0, to, at] = (re * scale[a]).astype(jnp.bfloat16)
                mat[1, to, at] = (im * scale[a]).astype(jnp.bfloat16)
            return 0

        lax.fori_loop(0, 8, pairs, 0)
        if lo == 0:
            table.wait()
        part = slice(32 * lo, 32 * hi)
        for k, (col, at, many) in enumerate(CHUNKS):
            even, odd = [
                jnp.dot(
                    mat[i, part, :], inv[i, :, col : col + 256], preferred_element_type=jnp.float32
                )
                for i in range(2)
            ]
            ahead = (even - odd).astype(jnp.bfloat16)
            back = (even + odd).astype(jnp.bfloat16)
            for i in range(lo, hi):
                to = slice(32 * (i - lo), 32 * (i - lo) + 32)
                if k == 0:
                    sbuf[i, 0:32], sbuf[i, 32:64] = ahead[to, 0:128], ahead[to, 128:256]
                    sbuf[i, 64:96], sbuf[i, 96:128] = back[to, 0:128], back[to, 128:256]
                else:
                    sbuf[i, 128:160], sbuf[i, 160:192] = ahead[to, 0:128], back[to, 0:128]
                    ends = jnp.where(
                        lax.broadcasted_iota(jnp.int32, (32, 128), 1) // 32 % 2 == 0,
                        ahead[to, 128:256].astype(jnp.float32),
                        back[to, 128:256].astype(jnp.float32),
                    )
                    sbuf[i, 192:208] = jnp.where(low, ends[0:16], ends[16:32]).astype(jnp.bfloat16)
                if i != 5:
                    start(
                        remote(sbuf.at[i, pl.ds(at, many)], rbuf.at[mine, pl.ds(at, many)],
                               s_o.at[k, i], r_o.at[k, mine], plane((me + i + 3) % 8))
                    )
    keep = pltpu.make_async_copy(sbuf.at[5], rbuf.at[mine], tsem)
    keep.start()
    keep.wait()
    q, lane = [lax.broadcasted_iota(jnp.int32, (128, 128), i) for i in range(2)]
    ends = q // 64 * 64 + jnp.where(q % 64 < 32, 48 - q % 64, q % 64 - 32)
    ahead, back, ends = [
        jnp.where(lane == to, 1.0, 0.0).astype(jnp.bfloat16) for to in (q, 127 - q, ends)
    ]

    def turned_block(n, at, order):
        for s in range(8):
            for cc in range(2):
                to = s // 4 * 64 + s // 2 % 2 * 4 + s % 2 + cc * 2
                v = rbuf[s, at + 8 * cc : at + 8 * cc + 8, :]
                turn_buf[n, pl.ds(to, 8, stride=8), :] = v.astype(jnp.float32)
        return lax.dot_general(
            order, turn_buf[n, 0:128, :].astype(jnp.bfloat16), (((1,), (1,)), ((), ())),
            preferred_element_type=jnp.float32,
        )

    for k, (_, at, many) in enumerate(CHUNKS):
        for d in range(1, 8):
            s = slot_of((me + d) % 8)
            remote(sbuf.at[0, pl.ds(at, many)], rbuf.at[s, pl.ds(at, many)],
                   s_o.at[k, 0], r_o.at[k, s], sibling).wait_recv()
        for a in range(2):
            for n in (0, 1) if k == 0 else (2,):
                to = MAXLAG - 128 * n
                out_ref[to - 127 : to + 1, a, :] = turned_block(
                    4 * n + 2 * a, (64, 96, 160)[n] + 16 * a, back
                )
                to = MAXLAG + 128 * n
                out_ref[to : to + 128, a, :] = turned_block(
                    4 * n + 2 * a + 1, (0, 32, 128)[n] + 16 * a, ahead
                )
        if k == 1:
            v = turned_block(12, 192, ends)
            for a in range(2):
                out_ref[0:17, a, :] = v[64 * a : 64 * a + 17]
                out_ref[784:801, a, :] = v[64 * a + 32 : 64 * a + 49]
    for copy in sent:
        copy.wait_send()


def on_device(traces, response_re, response_im, station_net, quality):
    twiddle, outer, inverse = tables()
    f32, bf16 = jnp.float32, jnp.bfloat16
    dma = pltpu.SemaphoreType.DMA
    lags = pl.pallas_call(
        kernel,
        out_shape=jax.ShapeDtypeStruct((LAGS, 2, 128), f32),
        in_specs=[pl.BlockSpec(memory_space=pltpu.HBM)] * 8,
        out_specs=pl.BlockSpec(memory_space=pltpu.VMEM),
        scratch_shapes=[
            pltpu.SMEM(station_net.shape, jnp.int32),
            pltpu.SMEM(quality.shape, jnp.int32),
            pltpu.VMEM(traces.shape, f32),
            pltpu.VMEM(twiddle.shape, f32),
            pltpu.VMEM(outer.shape, f32),
            pltpu.VMEM(inverse.shape, bf16),
            pltpu.VMEM((10, 8, 128), f32),
            pltpu.VMEM((128, 256), f32),
            pltpu.VMEM((136, 128), f32),
            pltpu.VMEM((128, 128), f32),
            pltpu.VMEM((2, 40, 128), f32),
            pltpu.VMEM((2, 40, 128), f32),
            pltpu.VMEM((2, 8, 16, 128), f32),
            pltpu.VMEM((8, 8, 128), jnp.int32),
            pltpu.VMEM((8, 16, 128), f32),
            pltpu.VMEM((8, 16, 128), f32),
            pltpu.VMEM((16, 1, 128), f32),
            pltpu.VMEM((2, 8, 1, 128), f32),
            pltpu.VMEM((16, 4, 16, 128), bf16),
            pltpu.VMEM((2, 8, 4, 16, 128), bf16),
            pltpu.VMEM((4, 272, 128), f32),
            pltpu.VMEM((16, 4, 16, 128), f32),
            pltpu.VMEM((8, 4, 2, 16, 128), f32),
            pltpu.VMEM((16, 128), f32),
            pltpu.VMEM((16, 16, 128), f32),
            pltpu.VMEM((2, 256, BINS), bf16),
            pltpu.VMEM((8, ROWS, 128), bf16),
            pltpu.VMEM((8, ROWS, 128), bf16),
            pltpu.VMEM((13, 136, 128), f32),
            dma((7,)), dma, dma((2,)), dma((2,)), dma((8,)), dma((8,)), dma((8,)), dma((8,)),
            dma((3,)), dma((3,)), dma((8,)), dma((8,)), dma((16,)), dma((16,)), dma((8,)), dma((8,)),
            dma((16,)), dma((16,)), dma((8,)), dma((8,)), dma((2, 8)), dma((2, 8)),
        ],
        compiler_params=pltpu.CompilerParams(
            collective_id=0, has_side_effects=True, vmem_limit_bytes=40 << 20
        ),
    )(
        *(
            pltpu.with_memory_space_constraint(v, pltpu.HBM)
            for v in (
                station_net, quality, traces, response_re.reshape(8, 128),
                response_im.reshape(8, 128), jnp.asarray(twiddle), jnp.asarray(outer),
                jnp.asarray(inverse),
            )
        )
    )
    return lags.transpose(1, 2, 0)


def solution(mesh):
    return jax.shard_map(
        on_device,
        mesh=mesh,
        in_specs=(P("sta", "win"), P("sta", None), P("sta", None), P("sta"), P("sta", "win")),
        out_specs=P("sta", "win", None),
        check_vma=False,
    )
```
